32 devices in a mesh: inner: 4 (over x, core), outer: 8 (over z, y).
Axes of the slice: x: 2, y: 2, z: 4, core: 2. Of those that a mesh axis runs over, the one named last changes fastest.
Arguments:
- queries: bfloat16 [4096, 2048], P(('outer', 'inner')), may hold values from -6 to 6
- keys: bfloat16 [4096, 2048], P(('outer', 'inner')), may hold values from -6 to 6
- values: bfloat16 [4096, 2048], P(('outer', 'inner')), may hold values from -6 to 6
- out_grad: bfloat16 [4096, 2048], P(('outer', 'inner')), may hold values from -6 to 6
- positions: int32 [4096], P(('outer', 'inner')), may hold values from 0 to 8191
Outputs:
- attended: bfloat16 [4096, 2048], P(('outer', 'inner'))
- query_grad: bfloat16 [4096, 2048], P(('outer', 'inner'))
- key_grad: bfloat16 [4096, 2048], P(('outer', 'inner'))
- value_gradient: bfloat16 [4096, 2048], P(('outer', 'inner'))
The draws below stay inside these ranges and needn't reach their ends.
All inputs are finite; a program needn't handle non-finite values.
Results may differ from the reference program's by a relative error of at most 0.0064.
Values sent between devices are 32-bit elements; how exact they have to be, the bound alone decides.
No kernel may reach another device: no remote copies, remote signals or barrier semaphores. Data moves between devices by JAX's collectives and lax.ppermute only.
A program may use at most 256 MiB of HBM per device.

```python
import math
import jax
import jax.numpy as jnp
from jax import lax

HEADS = 16
D_HEAD = 128
TOK_DEV = 128
TOKENS = 4096


def plant(array, rng, low, largest):
    longest = array.shape.index(max(array.shape))
    spots = []
    for shift in (0, 1):
        where = [jax.random.randint(jax.random.fold_in(rng, axis), (), 0, length) for axis, length in enumerate(array.shape)]
        where[longest] = (where[longest] + shift) % array.shape[longest]
        spots.append(tuple(where))
    return array.at[spots[0]].set(low).at[spots[1]].set(largest)


def block_scale(rng, extent, shards, smallest, largest):
    level = 1.0
    for position, parts in shards:
        heights = jax.random.uniform(jax.random.fold_in(jax.random.fold_in(rng, 6), position), (parts,), jnp.float32, smallest / len(shards), largest / len(shards))
        level = level * jnp.repeat(jnp.exp(heights), extent[position] // parts).reshape((-1,) + (1,) * (len(extent) - 1 - position))
    return level


def scatter_about(own_key, extent, scale, most, cuts=(), dtype=jnp.bfloat16):
    result = scale * jax.random.normal(own_key, extent, jnp.float32)
    if cuts:
        result = result * block_scale(own_key, extent, cuts, -0.22, 0.18)
    return jnp.clip(result, -most, most).astype(dtype)


def setup_inputs(seed: int = 0) -> dict:
    seeds = jax.random.split(jax.random.key(seed), 6)
    queries = scatter_about(seeds[0], (TOKENS, HEADS * D_HEAD), 1.0, 6.0, ((0, 32),))
    keys = scatter_about(seeds[1], (TOKENS, HEADS * D_HEAD), 1.0, 6.0, ((0, 32),))
    values = scatter_about(seeds[2], (TOKENS, HEADS * D_HEAD), 1.0, 6.0, ((0, 32),))
    out_grad = scatter_about(seeds[3], (TOKENS, HEADS * D_HEAD), 1.0, 6.0, ((0, 32),))
    positions = plant(jax.random.randint(seeds[4], (TOKENS,), 0, 8192), jax.random.fold_in(seeds[4], 1), 0, 8191).astype(jnp.int32)
    return dict(queries=queries, keys=keys, values=values, out_grad=out_grad, positions=positions)


def rotary_tables(positions, head_dim):
    half_dim = head_dim // 2
    spacing = jnp.arange(half_dim).astype(jnp.float32) * (-2.0 * math.log(500000.0) / head_dim)
    angle = positions.astype(jnp.float32)[:, None] * jnp.exp(spacing)[None, :]
    return jnp.cos(angle)[:, None, :], jnp.sin(angle)[:, None, :]


def rotate(rows, cosine, sine):
    half_dim = rows.shape[-1] // 2
    first = rows[..., :half_dim].astype(jnp.float32)
    second = rows[..., half_dim:].astype(jnp.float32)
    return jnp.concatenate([first * cosine - second * sine, second * cosine + first * sine], axis=-1)


def unrotate(rows, cosine, sine):
    half_dim = rows.shape[-1] // 2
    first = rows[..., :half_dim]
    second = rows[..., half_dim:]
    return jnp.concatenate([first * cosine + second * sine, second * cosine - first * sine], axis=-1)


def block_state(pair):
    left_operand, right_operand = pair
    return jnp.einsum("pob,poj->obj", left_operand.astype(jnp.float32), right_operand.astype(jnp.float32))


def reference(queries, keys, values, out_grad, positions):
    scale_factor = (D_HEAD * TOKENS) ** -0.5
    blocks = TOKENS // TOK_DEV
    shaped = (blocks, TOK_DEV, HEADS, D_HEAD)
    cosine, sine = rotary_tables(positions, D_HEAD)
    rotated_query = rotate(queries.reshape(TOKENS, HEADS, D_HEAD), cosine, sine).astype(jnp.bfloat16).reshape(shaped)
    rotated_key = rotate(keys.reshape(TOKENS, HEADS, D_HEAD), cosine, sine).astype(jnp.bfloat16).reshape(shaped)
    value_row_block = values.reshape(shaped)
    gradient_row_block = out_grad.reshape(shaped)
    cos_blocks = cosine.reshape(blocks, TOK_DEV, 1, D_HEAD // 2)
    sin_blocks = sine.reshape(blocks, TOK_DEV, 1, D_HEAD // 2)
    key_value_state = lax.map(block_state, (rotated_key, value_row_block))
    query_state = lax.map(block_state, (rotated_query, gradient_row_block))
    preceding_state = (jnp.cumsum(key_value_state, axis=0) - key_value_state).astype(jnp.bfloat16)
    following_state = (jnp.cumsum(query_state[::-1], axis=0)[::-1] - query_state).astype(jnp.bfloat16)
    causal = jnp.arange(TOK_DEV)[:, None] >= jnp.arange(TOK_DEV)[None, :]

    def one_block(items):
        qrot, krot, vrow, grow, cosb, sinb, before, after = items
        query_float = qrot.astype(jnp.float32)
        key_float = krot.astype(jnp.float32)
        value_float = vrow.astype(jnp.float32)
        gradient_float = grow.astype(jnp.float32)
        second_operand = before.astype(jnp.float32)
        first_operand = after.astype(jnp.float32)
        score_matrix = jnp.where(causal[None], jnp.einsum("thd,shd->hts", query_float, key_float), 0.0).astype(jnp.bfloat16).astype(jnp.float32)
        score_gradient = jnp.where(causal[None], jnp.einsum("thd,shd->hts", gradient_float, value_float), 0.0).astype(jnp.bfloat16).astype(jnp.float32)
        attended = scale_factor * (jnp.einsum("rgb,brf->grf", score_matrix, value_float) + jnp.einsum("axz,xzo->axo", query_float, second_operand))
        rotated_query_gradient = scale_factor * (jnp.einsum("rgb,brf->grf", score_gradient, key_float) + jnp.einsum("xge,gme->xgm", gradient_float, second_operand))
        rotated_key_gradient = scale_factor * (jnp.einsum("uox,oul->xul", score_gradient, query_float) + jnp.einsum("olb,lfb->olf", value_float, first_operand))
        value_gradient = scale_factor * (jnp.einsum("uox,oul->xul", score_matrix, gradient_float) + jnp.einsum("tyg,yge->tye", key_float, first_operand))
        return (attended.astype(jnp.bfloat16), unrotate(rotated_query_gradient, cosb, sinb).astype(jnp.bfloat16),
                unrotate(rotated_key_gradient, cosb, sinb).astype(jnp.bfloat16), value_gradient.astype(jnp.bfloat16))

    results = lax.map(one_block, (rotated_query, rotated_key, value_row_block, gradient_row_block, cos_blocks, sin_blocks, preceding_state, following_state))
    flat = (TOKENS, HEADS * D_HEAD)
    return (results[0].reshape(flat), results[1].reshape(flat), results[2].reshape(flat), results[3].reshape(flat))
```

```python
import functools
import math

import jax
import jax.numpy as jnp
from jax import lax
from jax.experimental import pallas as pl
from jax.experimental.pallas import tpu as pltpu
from jax.sharding import Mesh, PartitionSpec as P

D = 128
F32 = jnp.float32
BF16 = jnp.bfloat16
VMEM_LIMIT = 24 * 1024 * 1024


def rotary_tables(positions):
    half = D // 2
    spacing = jnp.arange(half).astype(F32) * (-2.0 * math.log(500000.0) / D)
    spacing = jnp.concatenate([spacing, spacing])
    sign = jnp.concatenate([-jnp.ones((half,), F32), jnp.ones((half,), F32)])
    angle = positions.astype(F32)[:, None] * jnp.exp(spacing)[None, :]
    return jnp.cos(angle), jnp.sin(angle) * sign[None, :]


def rotate(rows, cosine, sine):
    wide = rows.astype(F32)
    return wide * cosine + pltpu.roll(wide, D // 2, 1) * sine


def unrotate(rows, cosine, sine):
    return rows * cosine - pltpu.roll(rows, D // 2, 1) * sine


def dot(a, b, ca, cb):
    return lax.dot_general(a, b, (((ca,), (cb,)), ((), ())), preferred_element_type=F32)


def states_kernel(half_ref, q_ref, k_ref, v_ref, g_ref, cos_ref, sin_ref, out_ref):
    del half_ref
    cosine, sine = cos_ref[...], sin_ref[...]
    for h in range(out_ref.shape[0]):
        cols = slice(h * D, (h + 1) * D)
        krot = rotate(k_ref[:, cols], cosine, sine).astype(BF16)
        qrot = rotate(q_ref[:, cols], cosine, sine).astype(BF16)
        out_ref[h, 0] = dot(krot, v_ref[:, cols], 0, 0)
        out_ref[h, 1] = dot(qrot, g_ref[:, cols], 0, 0)


def states(half, q, k, v, g, cosine, sine, heads):
    rows = q.shape[0]
    steps = 2
    per = heads // steps
    wide = pl.BlockSpec((rows, per * D), lambda i, half: (0, half[0] * steps + i))
    table = pl.BlockSpec((rows, D), lambda i, half: (0, 0))
    return pl.pallas_call(
        states_kernel,
        grid_spec=pltpu.PrefetchScalarGridSpec(
            num_scalar_prefetch=1,
            grid=(steps,),
            in_specs=[wide] * 4 + [table] * 2,
            out_specs=pl.BlockSpec((per, 2, D, D), lambda i, half: (i, 0, 0, 0)),
        ),
        out_shape=jax.ShapeDtypeStruct((heads, 2, D, D), F32),
        compiler_params=pltpu.CompilerParams(vmem_limit_bytes=VMEM_LIMIT),
        cost_estimate=pl.CostEstimate(
            flops=4 * heads * rows * D * D, bytes_accessed=4 * rows * heads * D * 2 + heads * 2 * D * D * 4,
            transcendentals=0,
        ),
        name="block_states",
    )(half, q, k, v, g, cosine, sine)


def local_kernel(q_ref, k_ref, v_ref, g_ref, cos_ref, sin_ref, rot_ref, sc_ref):
    cosine, sine = cos_ref[...], sin_ref[...]
    rows = q_ref.shape[0]
    keep = lax.broadcasted_iota(jnp.int32, (rows, rows), 0) >= lax.broadcasted_iota(
        jnp.int32, (rows, rows), 1
    )
    kept = lax.broadcasted_iota(jnp.int32, (rows, rows), 0) <= lax.broadcasted_iota(
        jnp.int32, (rows, rows), 1
    )
    for h in range(rot_ref.shape[0]):
        cols = slice(h * D, (h + 1) * D)
        krot = rotate(k_ref[:, cols], cosine, sine).astype(BF16)
        qrot = rotate(q_ref[:, cols], cosine, sine).astype(BF16)
        v, g = v_ref[:, cols], g_ref[:, cols]
        rot_ref[h, 0] = qrot
        rot_ref[h, 1] = krot
        sc_ref[h, 0] = jnp.where(keep, dot(qrot, krot, 1, 1), 0.0).astype(BF16)
        sc_ref[h, 1] = jnp.where(keep, dot(g, v, 1, 1), 0.0).astype(BF16)
        sc_ref[h, 2] = jnp.where(kept, dot(krot, qrot, 1, 1), 0.0).astype(BF16)
        sc_ref[h, 3] = jnp.where(kept, dot(v, g, 1, 1), 0.0).astype(BF16)


def local_scores(q, k, v, g, cosine, sine, heads):
    rows = q.shape[0]
    per = 4
    wide = pl.BlockSpec((rows, per * D), lambda i: (0, i))
    table = pl.BlockSpec((rows, D), lambda i: (0, 0))
    return pl.pallas_call(
        local_kernel,
        grid=(heads // per,),
        in_specs=[wide] * 4 + [table] * 2,
        out_specs=[
            pl.BlockSpec((per, 2, rows, D), lambda i: (i, 0, 0, 0)),
            pl.BlockSpec((per, 4, rows, rows), lambda i: (i, 0, 0, 0)),
        ],
        out_shape=[
            jax.ShapeDtypeStruct((heads, 2, rows, D), BF16),
            jax.ShapeDtypeStruct((heads, 4, rows, rows), BF16),
        ],
        compiler_params=pltpu.CompilerParams(vmem_limit_bytes=VMEM_LIMIT),
        cost_estimate=pl.CostEstimate(
            flops=8 * heads * rows * D * D, bytes_accessed=10 * rows * heads * D * 2, transcendentals=0
        ),
        name="local_scores",
    )(q, k, v, g, cosine, sine)


def outputs_kernel(scale, prior, half_ref, st_ref, rot_ref, sc_ref, v_ref, g_ref, cos_ref, sin_ref, *refs):
    del half_ref
    att_ref, qg_ref, kg_ref, vg_ref = refs[prior:]
    cosine, sine = cos_ref[...], sin_ref[...]
    for h in range(rot_ref.shape[0]):
        cols = slice(h * D, (h + 1) * D)
        v, g = v_ref[:, cols], g_ref[:, cols]
        qrot, krot = rot_ref[h, 0], rot_ref[h, 1]
        before = st_ref[h, 0].astype(BF16)
        after = st_ref[h, 1].astype(BF16)
        att = dot(sc_ref[h, 0], v, 1, 0) + dot(qrot, before, 1, 0)
        rqg = dot(sc_ref[h, 1], krot, 1, 0) + dot(g, before, 1, 1)
        rkg = dot(sc_ref[h, 3], qrot, 1, 0) + dot(v, after, 1, 1)
        vg = dot(sc_ref[h, 2], g, 1, 0) + dot(krot, after, 1, 0)
        att_ref[:, cols] = (scale * att).astype(BF16)
        qg_ref[:, cols] = unrotate(scale * rqg, cosine, sine).astype(BF16)
        kg_ref[:, cols] = unrotate(scale * rkg, cosine, sine).astype(BF16)
        vg_ref[:, cols] = (scale * vg).astype(BF16)


def outputs(scale, half, st, rot, sc, v, g, cosine, sine, prior):
    rows, width = v.shape
    heads = st.shape[0]
    steps = 2
    per = heads // steps
    wide = pl.BlockSpec((rows, per * D), lambda i, half: (0, half[0] * steps + i))
    table = pl.BlockSpec((rows, D), lambda i, half: (0, 0))
    by_head = lambda i, half: (half[0] * steps + i, 0, 0, 0)
    return pl.pallas_call(
        functools.partial(outputs_kernel, scale, len(prior)),
        grid_spec=pltpu.PrefetchScalarGridSpec(
            num_scalar_prefetch=1,
            grid=(steps,),
            in_specs=[
                pl.BlockSpec((per, 2, D, D), lambda i, half: (i, 0, 0, 0)),
                pl.BlockSpec((per, 2, rows, D), by_head),
                pl.BlockSpec((per, 4, rows, rows), by_head),
                wide,
                wide,
                table,
                table,
            ]
            + [pl.BlockSpec(memory_space=pl.ANY)] * len(prior),
            out_specs=[wide] * 4,
        ),
        out_shape=[jax.ShapeDtypeStruct((rows, width), BF16)] * 4,
        input_output_aliases={8 + i: i for i in range(len(prior))},
        compiler_params=pltpu.CompilerParams(vmem_limit_bytes=VMEM_LIMIT),
        cost_estimate=pl.CostEstimate(
            flops=16 * heads * rows * D * D, bytes_accessed=12 * rows * heads * D * 2, transcendentals=0
        ),
        name="block_outputs",
    )(half, st, rot, sc, v, g, cosine, sine, *prior)


GROUP = ("zl", "y", "x")


def swap(value, axis):
    return lax.ppermute(value, axis, [(0, 1), (1, 0)])


def shards(q, k, v, g, positions):
    rows, width = q.shape
    heads = width // D
    part = heads // 2
    tokens = rows
    for axis in ("x", "core", "zh", "zl", "y"):
        tokens = tokens * lax.axis_size(axis)
    scale = (D * tokens) ** (-0.5)
    cosine, sine = rotary_tables(positions)
    core = lax.axis_index("core")
    mine, theirs = core.reshape(1), (1 - core).reshape(1)

    far = states(theirs, q, k, v, g, cosine, sine, part)
    near_other = swap(far, "core")
    near = states(mine, q, k, v, g, cosine, sine, part)
    chip = near + near_other

    members = lax.axis_size(GROUP)
    place = lax.axis_index(GROUP)
    cut = D * part // members
    pieces = chip.reshape(part, 2, D // cut, cut, D).swapaxes(1, 2).reshape(members, 2, cut, D)
    held = lax.all_to_all(pieces, GROUP, 0, 0, tiled=True)

    keys, queries = held[:, 0], held[:, 1]
    keys_all, queries_all = jnp.sum(keys, axis=0), jnp.sum(queries, axis=0)
    groups = lax.axis_size("zh")
    group = lax.axis_index("zh")
    if groups == 2:
        passed = swap(jnp.where(group == 0, keys_all, queries_all), "zh")
        keys_in = jnp.where(group == 1, passed, 0.0)
        queries_in = jnp.where(group == 0, passed, 0.0)
    else:
        both = lax.all_gather(jnp.stack([keys_all, queries_all]), "zh")
        order = jnp.arange(groups)[:, None, None]
        keys_in = jnp.sum(jnp.where(order < group, both[:, 0], 0.0), axis=0)
        queries_in = jnp.sum(jnp.where(order > group, both[:, 1], 0.0), axis=0)
    rot, sc = local_scores(q, k, v, g, cosine, sine, heads)
    before, total = [], keys_in
    for j in range(members):
        before.append(total)
        total = total + keys[j]
    after, total = [], queries_in
    for j in reversed(range(members)):
        after.insert(0, total)
        total = total + queries[j]
    back = jnp.stack([jnp.stack(before), jnp.stack(after)], axis=1)
    chip_state = lax.all_to_all(back, GROUP, 0, 0, tiled=True)
    chip_state = (
        chip_state.reshape(part, D // cut, 2, cut, D).swapaxes(1, 2).reshape(part, 2, D, D)
    )

    side = jnp.arange(2)[None, :, None, None]
    to_mine = chip_state + jnp.where(side == 1 - core, near_other, 0.0)
    to_theirs = chip_state + jnp.where(side == core, near, 0.0)
    far_state = swap(to_theirs, "core")
    first = outputs(scale, mine, to_mine, rot, sc, v, g, cosine, sine, ())
    return tuple(outputs(scale, theirs, far_state, rot, sc, v, g, cosine, sine, tuple(first)))


def solution(mesh):
    inner, outer = mesh.shape["inner"], mesh.shape["outer"]
    x = inner // 2
    y = x if outer % x == 0 else 1
    z = outer // y
    zl = 2 if z % 2 == 0 else 1
    whole = Mesh(mesh.devices.reshape(x, 2, z // zl, zl, y), ("x", "core", "zh", "zl", "y"))
    rows = ("zh", "zl", "y", "x", "core")
    return jax.shard_map(
        shards,
        mesh=whole,
        in_specs=(P(rows, None),) * 4 + (P(rows),),
        out_specs=(P(rows, None),) * 4,
        check_vma=False,
    )
```

```python
import functools
import math

import jax
import jax.numpy as jnp
from jax import lax
from jax.experimental import pallas as pl
from jax.experimental.pallas import tpu as pltpu
from jax.sharding import Mesh, PartitionSpec as P

D = 128
F32 = jnp.float32
BF16 = jnp.bfloat16
VMEM_LIMIT = 20 * 1024 * 1024
GROUP = ("zl", "y", "x")
CHUNKS = 1
HBM = pl.BlockSpec(memory_space=pltpu.HBM)
VMEM = pl.BlockSpec(memory_space=pltpu.VMEM)
SMEM = pl.BlockSpec(memory_space=pltpu.SMEM)


def in_hbm(shape):
    return pltpu.HBM(shape, F32)


def in_vmem(shape, dtype=F32):
    return pltpu.VMEM(shape, dtype)


def call(body, out_shape, in_specs, out_specs, scratch, flops, moved, name):
    return pl.pallas_call(
        body,
        out_shape=out_shape,
        in_specs=in_specs,
        out_specs=out_specs,
        scratch_shapes=scratch,
        compiler_params=pltpu.CompilerParams(vmem_limit_bytes=VMEM_LIMIT),
        cost_estimate=pl.CostEstimate(flops=flops, bytes_accessed=moved, transcendentals=0),
        name=name,
    )


def rotate(rows, cosine, sine):
    wide = rows.astype(F32)
    return wide * cosine + pltpu.roll(wide, D // 2, 1) * sine


def unrotate(rows, cosine, sine):
    return rows * cosine - pltpu.roll(rows, D // 2, 1) * sine


def dot(a, b, ca, cb):
    return lax.dot_general(a, b, (((ca,), (cb,)), ((), ())), preferred_element_type=F32)


def rotary_tables(positions):
    rows = positions.shape[1]
    half = D // 2
    lane = lax.broadcasted_iota(jnp.int32, (rows, D), 1)
    index = jnp.where(lane < half, lane, lane - half).astype(F32)
    frequency = jnp.exp(index * (-2.0 * math.log(500000.0) / D))
    place = jnp.broadcast_to(positions.astype(F32), (D, rows)).T
    angle = place * frequency
    sine = jnp.sin(angle)
    return jnp.cos(angle), jnp.where(lane < half, -sine, sine)


def states_body(first, chunk, heads, *refs):
    if first:
        half, pos, q, k, v, g, cos_ref, sin_ref, out_ref, qs, ks, vs, gs, sems = refs
    else:
        half, cos_ref, sin_ref, q, k, v, g, out_ref, qs, ks, vs, gs, sems = refs
    part = q.shape[1] // D // 2
    start = pl.multiple_of((half[0] * part + chunk * heads) * D, heads * D)
    copies = []
    for i, (src, dst) in enumerate(((k, ks), (v, vs), (q, qs), (g, gs))):
        copies.append(pltpu.make_async_copy(src.at[:, pl.ds(start, heads * D)], dst, sems.at[i]))
    for copy in copies:
        copy.start()
    if first:
        cosine, sine = rotary_tables(pos[...])
        cos_ref[...] = cosine
        sin_ref[...] = sine
    else:
        cosine, sine = cos_ref[...], sin_ref[...]
    per, cut = out_ref.shape[0] // heads, out_ref.shape[2]
    for side, (rows, others) in enumerate(((ks, vs), (qs, gs))):
        copies[2 * side].wait()
        copies[2 * side + 1].wait()
        for h in range(heads):
            cols = slice(h * D, (h + 1) * D)
            turned = rotate(rows[:, cols], cosine, sine).astype(BF16)
            state = dot(turned, others[:, cols], 0, 0)
            for i in range(per):
                out_ref[h * per + i, side] = state[i * cut : (i + 1) * cut]


def states(half, chunk, heads, members, q, k, v, g, tables, pos):
    rows = q.shape[0]
    cut = heads * D // members
    first = tables is None
    table = in_vmem((rows, D))
    result = in_vmem((members, 2, cut, D))
    body = functools.partial(states_body, first, chunk, heads)
    scratch = [pltpu.VMEM((rows, heads * D), BF16)] * 4 + [pltpu.SemaphoreType.DMA((4,))]
    work = (4 * heads * rows * D * D, heads * D * (8 * rows + 8 * D))
    if first:
        return call(body, [table, table, result], [SMEM, VMEM] + [HBM] * 4, [VMEM] * 3, scratch, *work, "block_states")(
            half, pos, q, k, v, g
        )
    return call(body, result, [SMEM, VMEM, VMEM] + [HBM] * 4, VMEM, scratch, *work, "block_states")(
        half, *tables, q, k, v, g
    )


def add_body(core, a_ref, b_ref, out_ref, kept_ref, give_ref, held, sems):
    last = held.shape[0]
    copies = [
        pltpu.make_async_copy(b_ref.at[:, 1 - core[0]], kept_ref, sems.at[last]),
        pltpu.make_async_copy(a_ref.at[:, core[0]], give_ref, sems.at[last + 1]),
    ]
    for j in range(held.shape[0]):
        held[j] = a_ref[j] + b_ref[j]
        copy = pltpu.make_async_copy(held.at[j], out_ref.at[j], sems.at[j])
        copy.start()
        copies.append(copy)
    copies[0].start()
    copies[1].start()
    for copy in copies:
        copy.wait()


def add(core, a, b):
    size = math.prod(a.shape)
    one_side = in_hbm(a.shape[:1] + a.shape[2:])
    return call(
        add_body, [in_hbm(a.shape), one_side, one_side], [SMEM, VMEM, VMEM], [HBM] * 3,
        [pltpu.VMEM(a.shape, F32), pltpu.SemaphoreType.DMA((a.shape[0] + 2,))], size, size * 12, "chip_sum",
    )(core, a, b)


def scan_body(group, held_ref, out_ref, send_ref, held, sems):
    members = held.shape[0]
    copies = [pltpu.make_async_copy(held_ref.at[j], held.at[j], sems.at[j]) for j in range(members)]
    for copy in copies:
        copy.start()
    total = jnp.zeros(held.shape[2:], F32)
    for j in range(members):
        copies[j].wait()
        out_ref[j, 0] = total
        total = total + held[j, 0]
    keys = total
    total = jnp.zeros(held.shape[2:], F32)
    for j in reversed(range(members)):
        out_ref[j, 1] = total
        total = total + held[j, 1]
    if send_ref.shape[0] == 1:
        send_ref[0] = jnp.where(group[0] == 0, keys, total)
    else:
        send_ref[0] = keys
        send_ref[1] = total


def scan(group, held, kinds):
    size = math.prod(held.shape)
    return call(
        scan_body, [in_vmem(held.shape), in_vmem((kinds,) + held.shape[2:])], [SMEM, HBM], [VMEM, VMEM],
        [pltpu.VMEM(held.shape, F32), pltpu.SemaphoreType.DMA((held.shape[0],))], size, size * 8, "chip_scan",
    )(group, held)


def offset_body(sums_ref, passed_ref, out_ref, held, sems):
    copies = []
    for j in range(held.shape[0]):
        held[j] = sums_ref[j] + passed_ref[...]
        copy = pltpu.make_async_copy(held.at[j], out_ref.at[j], sems.at[j])
        copy.start()
        copies.append(copy)
    for copy in copies:
        copy.wait()


def offset(sums, passed):
    size = math.prod(sums.shape)
    return call(
        offset_body, in_hbm(sums.shape), [VMEM, VMEM], HBM,
        [pltpu.VMEM(sums.shape, F32), pltpu.SemaphoreType.DMA((sums.shape[0],))], size, size * 8, "group_sum",
    )(sums, passed)


def local_kernel(q_ref, k_ref, v_ref, g_ref, cos_ref, sin_ref, rot_ref, sc_ref):
    cosine, sine = cos_ref[...], sin_ref[...]
    rows = q_ref.shape[0]
    row = lax.broadcasted_iota(jnp.int32, (rows, rows), 0)
    col = lax.broadcasted_iota(jnp.int32, (rows, rows), 1)
    for h in range(rot_ref.shape[0]):
        cols = slice(h * D, (h + 1) * D)
        krot = rotate(k_ref[:, cols], cosine, sine).astype(BF16)
        qrot = rotate(q_ref[:, cols], cosine, sine).astype(BF16)
        v, g = v_ref[:, cols], g_ref[:, cols]
        rot_ref[h, 0] = qrot
        rot_ref[h, 1] = krot
        sc_ref[h, 0] = jnp.where(row >= col, dot(qrot, krot, 1, 1), 0.0).astype(BF16)
        sc_ref[h, 1] = jnp.where(row >= col, dot(g, v, 1, 1), 0.0).astype(BF16)
        sc_ref[h, 2] = jnp.where(row <= col, dot(krot, qrot, 1, 1), 0.0).astype(BF16)
        sc_ref[h, 3] = jnp.where(row <= col, dot(v, g, 1, 1), 0.0).astype(BF16)


def local_scores(q, k, v, g, cosine, sine, heads):
    rows = q.shape[0]
    per = 4
    wide = pl.BlockSpec((rows, per * D), lambda i: (0, i))
    table = pl.BlockSpec((rows, D), lambda i: (0, 0))
    return pl.pallas_call(
        local_kernel,
        grid=(heads // per,),
        in_specs=[wide] * 4 + [table] * 2,
        out_specs=[
            pl.BlockSpec((per, 2, rows, D), lambda i: (i, 0, 0, 0)),
            pl.BlockSpec((per, 4, rows, rows), lambda i: (i, 0, 0, 0)),
        ],
        out_shape=[
            jax.ShapeDtypeStruct((heads, 2, rows, D), BF16),
            jax.ShapeDtypeStruct((heads, 4, rows, rows), BF16),
        ],
        compiler_params=pltpu.CompilerParams(vmem_limit_bytes=VMEM_LIMIT),
        cost_estimate=pl.CostEstimate(
            flops=8 * heads * rows * D * D, bytes_accessed=10 * rows * heads * D * 2, transcendentals=0
        ),
        name="local_scores",
    )(q, k, v, g, cosine, sine)


def outputs_kernel(scale, prior, where, st_ref, ex_ref, rot_ref, sc_ref, v_ref, g_ref, cos_ref, sin_ref, *refs):
    att_ref, qg_ref, kg_ref, vg_ref = refs[prior:]
    cosine, sine = cos_ref[...], sin_ref[...]
    heads = rot_ref.shape[0]
    per, cut = st_ref.shape[0] // heads, st_ref.shape[2]
    for h in range(heads):
        cols = slice(h * D, (h + 1) * D)
        v, g = v_ref[:, cols], g_ref[:, cols]
        qrot, krot = rot_ref[h, 0], rot_ref[h, 1]

        def state(side):
            whole = st_ref[h * per : (h + 1) * per, side].reshape(D, D)
            extra = ex_ref[h * per : (h + 1) * per].reshape(D, D)
            return (whole + jnp.where(where[1] == side, extra, 0.0)).astype(BF16)

        before, after = state(0), state(1)
        att = dot(sc_ref[h, 0], v, 1, 0) + dot(qrot, before, 1, 0)
        rqg = dot(sc_ref[h, 1], krot, 1, 0) + dot(g, before, 1, 1)
        rkg = dot(sc_ref[h, 3], qrot, 1, 0) + dot(v, after, 1, 1)
        vg = dot(sc_ref[h, 2], g, 1, 0) + dot(krot, after, 1, 0)
        att_ref[:, cols] = (scale * att).astype(BF16)
        qg_ref[:, cols] = unrotate(scale * rqg, cosine, sine).astype(BF16)
        kg_ref[:, cols] = unrotate(scale * rkg, cosine, sine).astype(BF16)
        vg_ref[:, cols] = (scale * vg).astype(BF16)


def outputs(scale, where, chunk, chunks, st, extra, rot, sc, v, g, tables, prior):
    rows, width = v.shape
    heads = width // D // 2 // chunks
    steps = 2
    per = heads // steps
    cut = st.shape[0] // steps
    base = lambda i, where: (where[0] * chunks + chunk) * steps + i
    wide = pl.BlockSpec((rows, per * D), lambda i, where: (0, base(i, where)))
    table = pl.BlockSpec((rows, D), lambda i, where: (0, 0))
    by_head = lambda i, where: (base(i, where), 0, 0, 0)
    return pl.pallas_call(
        functools.partial(outputs_kernel, scale, len(prior)),
        grid_spec=pltpu.PrefetchScalarGridSpec(
            num_scalar_prefetch=1,
            grid=(steps,),
            in_specs=[
                pl.BlockSpec((cut,) + st.shape[1:], lambda i, where: (i, 0, 0, 0)),
                pl.BlockSpec((cut,) + extra.shape[1:], lambda i, where: (i, 0, 0)),
                pl.BlockSpec((per, 2, rows, D), by_head),
                pl.BlockSpec((per, 4, rows, rows), by_head),
                wide,
                wide,
                table,
                table,
            ]
            + [pl.BlockSpec(memory_space=pl.ANY)] * len(prior),
            out_specs=[wide] * 4,
        ),
        out_shape=[jax.ShapeDtypeStruct((rows, width), BF16)] * 4,
        input_output_aliases={9 + i: i for i in range(len(prior))},
        compiler_params=pltpu.CompilerParams(vmem_limit_bytes=VMEM_LIMIT),
        cost_estimate=pl.CostEstimate(
            flops=16 * heads * rows * D * D, bytes_accessed=12 * rows * heads * D * 2, transcendentals=0
        ),
        name="block_outputs",
    )(where, st, extra, rot, sc, v, g, *tables, *prior)


def swap(value, axis):
    return lax.ppermute(value, axis, [(0, 1), (1, 0)])


def shards(q, k, v, g, positions):
    rows, width = q.shape
    heads = width // D
    part = heads // 2 // CHUNKS
    tokens = rows
    for axis in ("x", "core", "zh", "zl", "y"):
        tokens = tokens * lax.axis_size(axis)
    scale = (D * tokens) ** (-0.5)
    core, group = lax.axis_index("core"), lax.axis_index("zh")
    members, groups = lax.axis_size(GROUP), lax.axis_size("zh")
    mine, theirs = core.reshape(1), (1 - core).reshape(1)
    pos = positions.reshape(1, rows)
    chunks = range(CHUNKS)

    hq, hk, hv, hg = (pltpu.with_memory_space_constraint(a, pltpu.HBM) for a in (q, k, v, g))
    tables, far, near = None, [], []
    for c in chunks:
        made = states(theirs, c, part, members, hq, hk, hv, hg, tables, pos)
        if c == 0:
            tables, made = made[:2], made[2]
        far.append(made)
    near_other = [swap(value, "core") for value in far]
    for c in chunks:
        near.append(states(mine, c, part, members, hq, hk, hv, hg, tables, pos))
    chip, kept, give = zip(*(add(mine, near[c], near_other[c]) for c in chunks))
    chip, give, early = lax.optimization_barrier((chip, give, tables))
    held = [lax.all_to_all(chip[c], GROUP, 0, 0, tiled=True) for c in chunks]
    extra = [swap(give[c], "core") for c in chunks]
    rot, sc = local_scores(q, k, v, g, *early, heads)
    held, extra, rot, sc = lax.optimization_barrier((held, extra, rot, sc))

    back = []
    for c in chunks:
        sums, send = scan(group.reshape(1), held[c], 1 if groups == 2 else 2)
        side = jnp.arange(2)[:, None, None]
        if groups == 2:
            passed = jnp.where(side == 1 - group, swap(send, "zh"), 0.0)
        else:
            every = lax.all_gather(send, "zh")
            order = jnp.arange(groups)[:, None, None, None]
            wanted = jnp.where(side == 0, order < group, order > group)
            passed = jnp.sum(jnp.where(wanted, every, 0.0), axis=0)
        back.append(offset(sums, passed))
    whole = [lax.all_to_all(back[c], GROUP, 0, 0, tiled=True) for c in chunks]
    far_state = [swap(value, "core") for value in whole]

    slot = 1 - core
    made = ()
    for c in chunks:
        made = outputs(
            scale, jnp.stack([core, slot]), c, CHUNKS, whole[c], kept[c], rot, sc, v, g, tables, tuple(made)
        )
    for c in chunks:
        made = outputs(
            scale, jnp.stack([1 - core, slot]), c, CHUNKS, far_state[c], extra[c], rot, sc, v, g, tables, tuple(made)
        )
    return tuple(made)


def solution(mesh):
    inner, outer = mesh.shape["inner"], mesh.shape["outer"]
    x = inner // 2
    y = x if outer % x == 0 else 1
    z = outer // y
    zl = 2 if z % 2 == 0 else 1
    whole = Mesh(mesh.devices.reshape(x, 2, z // zl, zl, y), ("x", "core", "zh", "zl", "y"))
    rows = ("zh", "zl", "y", "x", "core")
    return jax.shard_map(
        shards,
        mesh=whole,
        in_specs=(P(rows, None),) * 4 + (P(rows),),
        out_specs=(P(rows, None),) * 4,
        check_vma=False,
    )
```

```python
import functools
import itertools
import math

import jax
import jax.numpy as jnp
from jax import lax
from jax.experimental import pallas as pl
from jax.experimental.pallas import tpu as pltpu
from jax.sharding import Mesh, PartitionSpec as P

D = 128
F32 = jnp.float32
BF16 = jnp.bfloat16
VMEM_LIMIT = 20 * 1024 * 1024
HBM = pl.BlockSpec(memory_space=pltpu.HBM)
VMEM = pl.BlockSpec(memory_space=pltpu.VMEM)
SMEM = pl.BlockSpec(memory_space=pltpu.SMEM)


def in_vmem(shape, dtype=F32):
    return pltpu.VMEM(shape, dtype)


def call(body, out_shape, in_specs, out_specs, scratch, flops, moved, name, aliases=None):
    return pl.pallas_call(
        body,
        out_shape=out_shape,
        in_specs=in_specs,
        out_specs=out_specs,
        scratch_shapes=scratch,
        input_output_aliases=aliases or {},
        compiler_params=pltpu.CompilerParams(vmem_limit_bytes=VMEM_LIMIT),
        cost_estimate=pl.CostEstimate(flops=flops, bytes_accessed=moved, transcendentals=0),
        name=name,
    )


def rotate(rows, cosine, sine):
    wide = rows.astype(F32)
    return wide * cosine + pltpu.roll(wide, D // 2, 1) * sine


def unrotate(rows, cosine, sine):
    return rows * cosine - pltpu.roll(rows, D // 2, 1) * sine


def dot(a, b, ca, cb):
    return lax.dot_general(a, b, (((ca,), (cb,)), ((), ())), preferred_element_type=F32)


def rotary_tables(positions):
    rows = positions.shape[1]
    half = D // 2
    lane = lax.broadcasted_iota(jnp.int32, (rows, D), 1)
    index = jnp.where(lane < half, lane, lane - half).astype(F32)
    frequency = jnp.exp(index * (-2.0 * math.log(500000.0) / D))
    place = jnp.broadcast_to(positions.astype(F32), (D, rows)).T
    angle = place * frequency
    sine = jnp.sin(angle)
    return jnp.cos(angle), jnp.where(lane < half, -sine, sine)


def states_body(first, far, heads, *refs):
    if first:
        core, _, _, pos, q, k, v, g, cos_ref, sin_ref, out_ref, ps, qs, ks, vs, gs, sems = refs
        pos_copy = pltpu.make_async_copy(pos, ps, sems.at[4])
        pos_copy.start()
    else:
        core, _, _, cos_ref, sin_ref, q, k, v, g, out_ref, qs, ks, vs, gs, sems = refs
    start = pl.multiple_of((1 - core[0] if far else core[0]) * (heads * D), heads * D)
    copies = []
    for i, (src, dst) in enumerate(((k, ks), (v, vs), (q, qs), (g, gs))):
        copies.append(pltpu.make_async_copy(src.at[:, pl.ds(start, heads * D)], dst, sems.at[i]))
    for copy in copies:
        copy.start()
    if first:
        pos_copy.wait()
        cosine, sine = rotary_tables(ps[...])
        cos_ref[...] = cosine
        sin_ref[...] = sine
    else:
        cosine, sine = cos_ref[...], sin_ref[...]
    per, cut = out_ref.shape[0] // heads, out_ref.shape[2]
    for side, (rows, others) in enumerate(((ks, vs), (qs, gs))):
        copies[2 * side].wait()
        copies[2 * side + 1].wait()
        for h in range(heads):
            cols = slice(h * D, (h + 1) * D)
            turned = rotate(rows[:, cols], cosine, sine).astype(BF16)
            state = dot(turned, others[:, cols], 0, 0)
            for i in range(per):
                out_ref[h * per + i, side] = state[i * cut : (i + 1) * cut]


def states(who, far, heads, members, q, k, v, g, tables, pos):
    rows = q.shape[0]
    first = tables is None
    table = in_vmem((rows, D))
    result = in_vmem((members, 2, heads * D // members, D))
    body = functools.partial(states_body, first, far, heads)
    scratch = [pltpu.VMEM((rows, heads * D), BF16)] * 4 + [pltpu.SemaphoreType.DMA((5,))]
    work = (4 * heads * rows * D * D, heads * D * (8 * rows + 8 * D))
    if first:
        return call(
            body, [table, table, result], [SMEM] * 3 + [HBM] * 5, [VMEM] * 3,
            [pltpu.VMEM((1, rows), jnp.int32)] + scratch, *work, "block_states",
        )(*who, pos, q, k, v, g)
    return call(body, result, [SMEM] * 3 + [VMEM, VMEM] + [HBM] * 4, VMEM, scratch, *work, "block_states")(
        *who, *tables, q, k, v, g
    )


def add_body(_, me, __, a_ref, b_ref, *pieces):
    me = me[0]
    for m, piece in enumerate(pieces):
        piece[...] = a_ref[me ^ m] + b_ref[me ^ m]


def add(who, a, b):
    members, _, cut, _ = a.shape
    return call(
        add_body, [in_vmem((2, cut, D))] * members, [SMEM] * 3 + [VMEM, VMEM],
        [VMEM] * members, [], a.size, a.size * 12, "chip_sum",
    )(*who, a, b)


def total_body(_, __, group, *refs):
    group = group[0]
    out_ref = refs[-1]
    for side in range(2):
        total = refs[0][side]
        for ref in refs[1:-1]:
            total = total + ref[side]
        if out_ref.shape[0] == 2:
            out_ref[side] = total
        elif side == 0:
            keys = total
        else:
            out_ref[0] = jnp.where(group == 0, keys, total)


def total(who, pieces, kinds):
    _, cut, _ = pieces[0].shape
    size = len(pieces) * pieces[0].size
    return call(
        total_body, in_vmem((kinds, cut, D)), [SMEM] * 3 + [VMEM] * len(pieces), VMEM, [], size, size * 4, "block_total",
    )(*who, *pieces)


def offset_body(members, _, __, group, passed_ref, *refs):
    group = group[0]
    for side in range(2):
        if passed_ref.shape[0] == 1:
            extra = jnp.where(group == 1 - side, passed_ref[0], 0.0)
        else:
            extra = passed_ref[side]
        for m in range(members):
            refs[members + m][side] = refs[m][side] + extra


def offset(who, sums, passed):
    members = len(sums)
    size = members * sums[0].size
    return call(
        functools.partial(offset_body, members), [in_vmem(sums[0].shape)] * members,
        [SMEM] * 3 + [VMEM] * (members + 1), [VMEM] * members, [], size, size * 8, "group_sum",
    )(*who, passed, *sums)


def scan_body(members, _, me, __, *refs):
    pieces, sums, (held, ran) = refs[:members], refs[members : 2 * members], refs[2 * members :]
    me = me[0]
    for m in range(members):
        held[me ^ m] = pieces[m][...]
    for side, order in enumerate((range(members), reversed(range(members)))):
        total = jnp.zeros(held.shape[2:], F32)
        for j in order:
            ran[j, side] = total
            total = total + held[j, side]
    for m in range(members):
        sums[m][...] = ran[me ^ m]


def scan(who, pieces):
    members, (_, cut, _) = len(pieces), pieces[0].shape
    shape = (members, 2, cut, D)
    size = math.prod(shape)
    return call(
        functools.partial(scan_body, members), [in_vmem((2, cut, D))] * members,
        [SMEM] * 3 + [VMEM] * members, [VMEM] * members, [pltpu.VMEM(shape, F32)] * 2, size, size * 8, "chip_scan",
    )(*who, *pieces)


def local_kernel(q_ref, k_ref, v_ref, g_ref, cos_ref, sin_ref, rot_ref, sc_ref):
    cosine, sine = cos_ref[...], sin_ref[...]
    rows = q_ref.shape[0]
    row = lax.broadcasted_iota(jnp.int32, (rows, rows), 0)
    col = lax.broadcasted_iota(jnp.int32, (rows, rows), 1)
    for h in range(rot_ref.shape[0]):
        cols = slice(h * D, (h + 1) * D)
        krot = rotate(k_ref[:, cols], cosine, sine).astype(BF16)
        qrot = rotate(q_ref[:, cols], cosine, sine).astype(BF16)
        v, g = v_ref[:, cols], g_ref[:, cols]
        rot_ref[h, 0] = qrot
        rot_ref[h, 1] = krot
        rot_ref[h, 2] = v
        rot_ref[h, 3] = g
        sc_ref[h, 0] = jnp.where(row >= col, dot(qrot, krot, 1, 1), 0.0).astype(BF16)
        sc_ref[h, 1] = jnp.where(row >= col, dot(g, v, 1, 1), 0.0).astype(BF16)
        sc_ref[h, 2] = jnp.where(row <= col, dot(krot, qrot, 1, 1), 0.0).astype(BF16)
        sc_ref[h, 3] = jnp.where(row <= col, dot(v, g, 1, 1), 0.0).astype(BF16)


def local_scores(q, k, v, g, cosine, sine, heads):
    rows = q.shape[0]
    return call(
        local_kernel,
        [in_vmem((heads, 4, rows, D), BF16), in_vmem((heads, 4, rows, rows), BF16)],
        [VMEM] * 6, [VMEM] * 2, [], 8 * heads * rows * D * D, 10 * rows * heads * D * 2, "local_scores",
    )(q, k, v, g, cosine, sine)


def outputs_body(scale, per, heads, far, core, me, _, rot_ref, sc_ref, cos_ref, sin_ref, *refs):
    core, me = core[0], me[0]
    count = heads * per
    if far:
        pieces, refs = refs[:1], refs[5:]
    else:
        extra_ref, pieces, refs = refs[0], refs[1 : 1 + count], refs[1 + count :]
    outs, (state_ref, held, sems) = refs[:4], refs[4:]
    cosine, sine = cos_ref[...], sin_ref[...]
    copies = []
    for n in range(heads):
        low = me % per
        head = (me // per) ^ n
        for i in range(per):
            cut = pieces[0].shape[-2]
            at = pl.ds(pl.multiple_of((low ^ i) * cut, cut), cut)
            for side in range(2):
                if far:
                    state = pieces[0][n * per + i, side]
                else:
                    extra = extra_ref[head * per + (low ^ i), side]
                    state = pieces[n * per + i][side] + jnp.where(core == 1 - side, extra, 0.0)
                state_ref[n, side, at] = state.astype(BF16)
        before, after = state_ref[n, 0], state_ref[n, 1]
        at = (1 - core if far else core) * heads + head
        qrot, krot, v, g = (rot_ref[at, i] for i in range(4))
        att = dot(sc_ref[at, 0], v, 1, 0) + dot(qrot, before, 1, 0)
        rqg = dot(sc_ref[at, 1], krot, 1, 0) + dot(g, before, 1, 1)
        rkg = dot(sc_ref[at, 3], qrot, 1, 0) + dot(v, after, 1, 1)
        vg = dot(sc_ref[at, 2], g, 1, 0) + dot(krot, after, 1, 0)
        held[n, 0] = (scale * att).astype(BF16)
        held[n, 1] = unrotate(scale * rqg, cosine, sine).astype(BF16)
        held[n, 2] = unrotate(scale * rkg, cosine, sine).astype(BF16)
        held[n, 3] = (scale * vg).astype(BF16)
        for i in range(4):
            cols = pl.ds(pl.multiple_of(at * D, D), D)
            copies.append(pltpu.make_async_copy(held.at[n, i], outs[i].at[:, cols], sems.at[n, i]))
            copies[-1].start()
    for copy in copies:
        copy.wait()


def outputs(scale, per, count, who, rot, sc, tables, extra, pieces, prior):
    heads, _, rows, _ = rot.shape
    far = extra is None
    pieces = list(pieces) if far else [extra, *pieces]
    return call(
        functools.partial(outputs_body, scale, per, count, far),
        [pltpu.HBM((rows, heads * D), BF16)] * 4,
        [SMEM] * 3 + [VMEM] * (4 + len(pieces)) + [HBM] * len(prior),
        [HBM] * 4,
        [
            pltpu.VMEM((count, 2, D, D), BF16),
            pltpu.VMEM((count, 4, rows, D), BF16),
            pltpu.SemaphoreType.DMA((count, 4)),
        ],
        16 * count * rows * D * D,
        12 * rows * count * D * 2,
        "block_outputs",
        {7 + len(pieces) + i: i for i in range(len(prior))},
    )(*who, rot, sc, *tables, *pieces, *prior)


def relay_body(masks, core, me, _, near_ref, *refs):
    core, me = core[0], me[0]
    out_ref = refs[-1]
    for n, mask in enumerate(masks):
        for side in range(2):
            own = jnp.where(core == side, near_ref[me ^ mask, side], 0.0)
            out_ref[n, side] = refs[n][side] + own


def relay(masks, who, near, pieces):
    size = len(pieces) * pieces[0].size
    return call(
        functools.partial(relay_body, masks), in_vmem((len(pieces),) + pieces[0].shape),
        [SMEM] * 3 + [VMEM] * (1 + len(pieces)), VMEM, [], size, size * 8, "sibling_state",
    )(*who, near, *pieces)


def swap(value, axis):
    return lax.ppermute(value, axis, [(0, 1), (1, 0)])


AXES = ("x", "zl", "y")


def send_to(value, mask):
    x, zl, y = (lax.axis_size(axis) for axis in AXES)
    mx, my, mz = mask % x, mask // x % y, mask // (x * y)
    place = lambda a, b, c: (a * zl + b) * y + c
    pairs = [
        (place(a, b, c), place(a ^ mx, b ^ mz, c ^ my))
        for a, b, c in itertools.product(range(x), range(zl), range(y))
    ]
    return lax.ppermute(value, AXES, pairs)


def barrier(*values):
    return lax.optimization_barrier(values)


def exchange(pieces, order):
    arrived = {m: send_to(pieces[m], m) for m in order}
    arrived[0] = pieces[0]
    return arrived


def shards(q, k, v, g, positions):
    rows, width = q.shape
    heads = width // D
    part = heads // 2
    tokens = rows
    for axis in ("x", "core", "zh", "zl", "y"):
        tokens = tokens * lax.axis_size(axis)
    scale = (D * tokens) ** (-0.5)
    core, group = lax.axis_index("core"), lax.axis_index("zh")
    members, groups = lax.axis_size(("zl", "y", "x")), lax.axis_size("zh")
    me = lax.axis_index(("zl", "y", "x"))
    who = [scalar.reshape(1) for scalar in (core, me, group)]
    per = members // part
    pos = positions.reshape(1, rows)

    hq, hk, hv, hg, pos = (pltpu.with_memory_space_constraint(a, pltpu.HBM) for a in (q, k, v, g, pos))
    *tables, far = states(who, True, part, members, hq, hk, hv, hg, None, pos)
    near_other = swap(far, "core")
    near = states(who, False, part, members, hq, hk, hv, hg, tables, pos)
    pieces = add(who, near, near_other)
    pieces, tables = barrier(pieces, tables)

    order = sorted(range(1, members), key=lambda m: (bin(m).count("1"), m))
    arrived = exchange(pieces, order)
    rot, sc = local_scores(q, k, v, g, *tables, heads)
    listed, rot, sc = barrier([arrived[m] for m in order], rot, sc)
    arrived = [pieces[0]] + [listed[order.index(m)] for m in range(1, members)]

    send = total(who, arrived, 1 if groups == 2 else 2)
    if groups == 2:
        passed = swap(send, "zh")
    else:
        every = lax.all_gather(send, "zh")
        place = jnp.arange(groups)[:, None, None, None]
        wanted = jnp.where(jnp.arange(2)[:, None, None] == 0, place < group, place > group)
        passed = jnp.sum(jnp.where(wanted, every, 0.0), axis=0)
    pieces = offset(who, scan(who, arrived), passed)
    whole = exchange(pieces, order)

    whole = barrier(*(whole[m] for m in range(members)))
    other = swap(relay(range(members), who, near, whole), "core")
    made = outputs(scale, per, part, who, rot, sc, tables, near_other, whole, ())
    made = outputs(scale, per, part, who, rot, sc, tables, None, [other], tuple(made))
    return tuple(made)


def solution(mesh):
    inner, outer = mesh.shape["inner"], mesh.shape["outer"]
    x = inner // 2
    y = x if outer % x == 0 else 1
    z = outer // y
    zl = 2 if z % 2 == 0 else 1
    whole = Mesh(mesh.devices.reshape(x, 2, z // zl, zl, y), ("x", "core", "zh", "zl", "y"))
    rows = ("zh", "zl", "y", "x", "core")
    return jax.shard_map(
        shards,
        mesh=whole,
        in_specs=(P(rows, None),) * 4 + (P(rows),),
        out_specs=(P(rows, None),) * 4,
        check_vma=False,
    )
```

```python
import functools
import itertools
import math

import jax
import jax.numpy as jnp
from jax import lax
from jax.experimental import pallas as pl
from jax.experimental.pallas import tpu as pltpu
from jax.sharding import Mesh, PartitionSpec as P

D = 128
F32 = jnp.float32
BF16 = jnp.bfloat16
VMEM_LIMIT = 20 * 1024 * 1024
HBM = pl.BlockSpec(memory_space=pltpu.HBM)
VMEM = pl.BlockSpec(memory_space=pltpu.VMEM)
SMEM = pl.BlockSpec(memory_space=pltpu.SMEM)


def in_vmem(shape, dtype=F32):
    return pltpu.VMEM(shape, dtype)


def call(body, out_shape, in_specs, out_specs, scratch, flops, moved, name, aliases=None):
    return pl.pallas_call(
        body,
        out_shape=out_shape,
        in_specs=in_specs,
        out_specs=out_specs,
        scratch_shapes=scratch,
        input_output_aliases=aliases or {},
        compiler_params=pltpu.CompilerParams(vmem_limit_bytes=VMEM_LIMIT),
        cost_estimate=pl.CostEstimate(flops=flops, bytes_accessed=moved, transcendentals=0),
        name=name,
    )


def rotate(rows, cosine, sine):
    wide = rows.astype(F32)
    return wide * cosine + pltpu.roll(wide, D // 2, 1) * sine


def unrotate(rows, cosine, sine):
    return rows * cosine - pltpu.roll(rows, D // 2, 1) * sine


def dot(a, b, ca, cb):
    return lax.dot_general(a, b, (((ca,), (cb,)), ((), ())), preferred_element_type=F32)


def rotary_tables(positions):
    rows = positions.shape[1]
    half = D // 2
    lane = lax.broadcasted_iota(jnp.int32, (rows, D), 1)
    index = jnp.where(lane < half, lane, lane - half).astype(F32)
    frequency = jnp.exp(index * (-2.0 * math.log(500000.0) / D))
    place = jnp.broadcast_to(positions.astype(F32), (D, rows)).T
    angle = place * frequency
    sine = jnp.sin(angle)
    return jnp.cos(angle), jnp.where(lane < half, -sine, sine)


def states_body(first, far, heads, *refs):
    if first:
        core, _, _, pos, q, k, v, g, cos_ref, sin_ref, out_ref, ps, qs, ks, vs, gs, sems = refs
        pos_copy = pltpu.make_async_copy(pos, ps, sems.at[4])
        pos_copy.start()
    else:
        core, _, _, cos_ref, sin_ref, q, k, v, g, out_ref, qs, ks, vs, gs, sems = refs
    start = pl.multiple_of((1 - core[0] if far else core[0]) * (heads * D), heads * D)
    copies = []
    for i, (src, dst) in enumerate(((k, ks), (v, vs), (q, qs), (g, gs))):
        copies.append(pltpu.make_async_copy(src.at[:, pl.ds(start, heads * D)], dst, sems.at[i]))
    for copy in copies:
        copy.start()
    if first:
        pos_copy.wait()
        cosine, sine = rotary_tables(ps[...])
        cos_ref[...] = cosine
        sin_ref[...] = sine
    else:
        cosine, sine = cos_ref[...], sin_ref[...]
    per, cut = out_ref.shape[0] // heads, out_ref.shape[2]
    for side, (rows, others) in enumerate(((ks, vs), (qs, gs))):
        copies[2 * side].wait()
        copies[2 * side + 1].wait()
        for h in range(heads):
            cols = slice(h * D, (h + 1) * D)
            turned = rotate(rows[:, cols], cosine, sine).astype(BF16)
            state = dot(turned, others[:, cols], 0, 0)
            for i in range(per):
                out_ref[h * per + i, side] = state[i * cut : (i + 1) * cut]


def states(who, far, heads, members, q, k, v, g, tables, pos):
    rows = q.shape[0]
    first = tables is None
    table = in_vmem((rows, D))
    result = in_vmem((members, 2, heads * D // members, D))
    body = functools.partial(states_body, first, far, heads)
    scratch = [pltpu.VMEM((rows, heads * D), BF16)] * 4 + [pltpu.SemaphoreType.DMA((5,))]
    work = (4 * heads * rows * D * D, heads * D * (8 * rows + 8 * D))
    if first:
        return call(
            body, [table, table, result], [SMEM] * 3 + [HBM] * 5, [VMEM] * 3,
            [pltpu.VMEM((1, rows), jnp.int32)] + scratch, *work, "block_states",
        )(*who, pos, q, k, v, g)
    return call(body, result, [SMEM] * 3 + [VMEM, VMEM] + [HBM] * 4, VMEM, scratch, *work, "block_states")(
        *who, *tables, q, k, v, g
    )


def add_body(_, me, __, a_ref, b_ref, *pieces):
    me = me[0]
    for m, piece in enumerate(pieces):
        piece[...] = a_ref[me ^ m] + b_ref[me ^ m]


def add(who, a, b):
    members, _, cut, _ = a.shape
    return call(
        add_body, [in_vmem((2, cut, D))] * members, [SMEM] * 3 + [VMEM, VMEM],
        [VMEM] * members, [], a.size, a.size * 12, "chip_sum",
    )(*who, a, b)


def total_body(_, __, group, *refs):
    group = group[0]
    out_ref = refs[-1]
    for side in range(2):
        total = refs[0][side]
        for ref in refs[1:-1]:
            total = total + ref[side]
        if out_ref.shape[0] == 2:
            out_ref[side] = total
        elif side == 0:
            keys = total
        else:
            out_ref[0] = jnp.where(group == 0, keys, total)


def total(who, pieces, kinds):
    _, cut, _ = pieces[0].shape
    size = len(pieces) * pieces[0].size
    return call(
        total_body, in_vmem((kinds, cut, D)), [SMEM] * 3 + [VMEM] * len(pieces), VMEM, [], size, size * 4, "block_total",
    )(*who, *pieces)


def offset_body(members, _, __, group, passed_ref, *refs):
    group = group[0]
    for side in range(2):
        if passed_ref.shape[0] == 1:
            extra = jnp.where(group == 1 - side, passed_ref[0], 0.0)
        else:
            extra = passed_ref[side]
        for m in range(members):
            refs[members + m][side] = refs[m][side] + extra


def offset(who, sums, passed):
    members = len(sums)
    size = members * sums[0].size
    return call(
        functools.partial(offset_body, members), [in_vmem(sums[0].shape)] * members,
        [SMEM] * 3 + [VMEM] * (members + 1), [VMEM] * members, [], size, size * 8, "group_sum",
    )(*who, passed, *sums)


def scan_body(members, _, me, __, *refs):
    pieces, sums, (held, ran) = refs[:members], refs[members : 2 * members], refs[2 * members :]
    me = me[0]
    for m in range(members):
        held[me ^ m] = pieces[m][...]
    for side, order in enumerate((range(members), reversed(range(members)))):
        total = jnp.zeros(held.shape[2:], F32)
        for j in order:
            ran[j, side] = total
            total = total + held[j, side]
    for m in range(members):
        sums[m][...] = ran[me ^ m]


def scan(who, pieces):
    members, (_, cut, _) = len(pieces), pieces[0].shape
    shape = (members, 2, cut, D)
    size = math.prod(shape)
    return call(
        functools.partial(scan_body, members), [in_vmem((2, cut, D))] * members,
        [SMEM] * 3 + [VMEM] * members, [VMEM] * members, [pltpu.VMEM(shape, F32)] * 2, size, size * 8, "chip_scan",
    )(*who, *pieces)


def local_kernel(q_ref, k_ref, v_ref, g_ref, cos_ref, sin_ref, rot_ref, sc_ref):
    cosine, sine = cos_ref[...], sin_ref[...]
    rows = q_ref.shape[0]
    row = lax.broadcasted_iota(jnp.int32, (rows, rows), 0)
    col = lax.broadcasted_iota(jnp.int32, (rows, rows), 1)
    for h in range(rot_ref.shape[0]):
        cols = slice(h * D, (h + 1) * D)
        krot = rotate(k_ref[:, cols], cosine, sine).astype(BF16)
        qrot = rotate(q_ref[:, cols], cosine, sine).astype(BF16)
        v, g = v_ref[:, cols], g_ref[:, cols]
        rot_ref[h, 0] = qrot
        rot_ref[h, 1] = krot
        rot_ref[h, 2] = v
        rot_ref[h, 3] = g
        sc_ref[h, 0] = jnp.where(row >= col, dot(qrot, krot, 1, 1), 0.0).astype(BF16)
        sc_ref[h, 1] = jnp.where(row >= col, dot(g, v, 1, 1), 0.0).astype(BF16)
        sc_ref[h, 2] = jnp.where(row <= col, dot(krot, qrot, 1, 1), 0.0).astype(BF16)
        sc_ref[h, 3] = jnp.where(row <= col, dot(v, g, 1, 1), 0.0).astype(BF16)


def local_scores(q, k, v, g, cosine, sine, heads):
    rows = q.shape[0]
    return call(
        local_kernel,
        [in_vmem((heads, 4, rows, D), BF16), in_vmem((heads, 4, rows, rows), BF16)],
        [VMEM] * 6, [VMEM] * 2, [], 8 * heads * rows * D * D, 10 * rows * heads * D * 2, "local_scores",
    )(q, k, v, g, cosine, sine)


def outputs_body(scale, per, heads, far, core, me, _, rot_ref, sc_ref, cos_ref, sin_ref, *refs):
    core, me = core[0], me[0]
    count = heads * per
    if far:
        pieces, refs = refs[:1], refs[5:]
    else:
        extra_ref, pieces, refs = refs[0], refs[1 : 1 + count], refs[1 + count :]
    outs, (state_ref, held, sems) = refs[:4], refs[4:]
    cosine, sine = cos_ref[...], sin_ref[...]
    copies = []
    for n in range(heads):
        low = me % per
        head = (me // per) ^ n
        for i in range(per):
            cut = pieces[0].shape[-2]
            at = pl.ds(pl.multiple_of((low ^ i) * cut, cut), cut)
            for side in range(2):
                if far:
                    state = pieces[0][n * per + i, side]
                else:
                    extra = extra_ref[head * per + (low ^ i), side]
                    state = pieces[n * per + i][side] + jnp.where(core == 1 - side, extra, 0.0)
                state_ref[n, side, at] = state.astype(BF16)
        before, after = state_ref[n, 0], state_ref[n, 1]
        at = (1 - core if far else core) * heads + head
        qrot, krot, v, g = (rot_ref[at, i] for i in range(4))
        att = dot(sc_ref[at, 0], v, 1, 0) + dot(qrot, before, 1, 0)
        rqg = dot(sc_ref[at, 1], krot, 1, 0) + dot(g, before, 1, 1)
        rkg = dot(sc_ref[at, 3], qrot, 1, 0) + dot(v, after, 1, 1)
        vg = dot(sc_ref[at, 2], g, 1, 0) + dot(krot, after, 1, 0)
        held[n, 0] = (scale * att).astype(BF16)
        held[n, 1] = unrotate(scale * rqg, cosine, sine).astype(BF16)
        held[n, 2] = unrotate(scale * rkg, cosine, sine).astype(BF16)
        held[n, 3] = (scale * vg).astype(BF16)
        for i in range(4):
            cols = pl.ds(pl.multiple_of(at * D, D), D)
            copies.append(pltpu.make_async_copy(held.at[n, i], outs[i].at[:, cols], sems.at[n, i]))
            copies[-1].start()
    for copy in copies:
        copy.wait()


def outputs(scale, per, count, who, rot, sc, tables, extra, pieces, prior):
    heads, _, rows, _ = rot.shape
    far = extra is None
    pieces = list(pieces) if far else [extra, *pieces]
    return call(
        functools.partial(outputs_body, scale, per, count, far),
        [pltpu.HBM((rows, heads * D), BF16)] * 4,
        [SMEM] * 3 + [VMEM] * (4 + len(pieces)) + [HBM] * len(prior),
        [HBM] * 4,
        [
            pltpu.VMEM((count, 2, D, D), BF16),
            pltpu.VMEM((count, 4, rows, D), BF16),
            pltpu.SemaphoreType.DMA((count, 4)),
        ],
        16 * count * rows * D * D,
        12 * rows * count * D * 2,
        "block_outputs",
        {7 + len(pieces) + i: i for i in range(len(prior))},
    )(*who, rot, sc, *tables, *pieces, *prior)


def relay_body(masks, core, me, _, near_ref, *refs):
    core, me = core[0], me[0]
    out_ref = refs[-1]
    for n, mask in enumerate(masks):
        for side in range(2):
            own = jnp.where(core == side, near_ref[me ^ mask, side], 0.0)
            out_ref[n, side] = refs[n][side] + own


def relay(masks, who, near, pieces):
    size = len(pieces) * pieces[0].size
    return call(
        functools.partial(relay_body, masks), in_vmem((len(pieces),) + pieces[0].shape),
        [SMEM] * 3 + [VMEM] * (1 + len(pieces)), VMEM, [], size, size * 8, "sibling_state",
    )(*who, near, *pieces)


def swap(value, axis):
    return lax.ppermute(value, axis, [(0, 1), (1, 0)])


AXES = ("x", "zl", "y")


def send_to(value, mask):
    x, zl, y = (lax.axis_size(axis) for axis in AXES)
    mx, my, mz = mask % x, mask // x % y, mask // (x * y)
    place = lambda a, b, c: (a * zl + b) * y + c
    pairs = [
        (place(a, b, c), place(a ^ mx, b ^ mz, c ^ my))
        for a, b, c in itertools.product(range(x), range(zl), range(y))
    ]
    return lax.ppermute(value, AXES, pairs)


def barrier(*values):
    return lax.optimization_barrier(values)


def exchange(pieces, order):
    arrived = {m: send_to(pieces[m], m) for m in order}
    arrived[0] = pieces[0]
    return arrived


def shards(q, k, v, g, positions):
    rows, width = q.shape
    heads = width // D
    part = heads // 2
    tokens = rows
    for axis in ("x", "core", "zh", "zl", "y"):
        tokens = tokens * lax.axis_size(axis)
    scale = (D * tokens) ** (-0.5)
    core, group = lax.axis_index("core"), lax.axis_index("zh")
    members, groups = lax.axis_size(("zl", "y", "x")), lax.axis_size("zh")
    me = lax.axis_index(("zl", "y", "x"))
    who = [scalar.reshape(1) for scalar in (core, me, group)]
    per = members // part
    pos = positions.reshape(1, rows)

    hq, hk, hv, hg, pos = (pltpu.with_memory_space_constraint(a, pltpu.HBM) for a in (q, k, v, g, pos))
    *tables, far = states(who, True, part, members, hq, hk, hv, hg, None, pos)
    near_other = swap(far, "core")
    near = states(who, False, part, members, hq, hk, hv, hg, tables, pos)
    pieces = add(who, near, near_other)
    pieces, tables = barrier(pieces, tables)

    order = []
    for m in sorted(range(1, members - 1), key=lambda m: (bin(m).count("1"), m))[: members // 2 - 1]:
        order += [m, members - 1 - m]
    order.append(members - 1)
    arrived = exchange(pieces, order)
    rot, sc = local_scores(q, k, v, g, *tables, heads)
    listed, rot, sc = barrier([arrived[m] for m in order], rot, sc)
    arrived = [pieces[0]] + [listed[order.index(m)] for m in range(1, members)]

    send = total(who, arrived, 1 if groups == 2 else 2)
    if groups == 2:
        passed = swap(send, "zh")
    else:
        every = lax.all_gather(send, "zh")
        place = jnp.arange(groups)[:, None, None, None]
        wanted = jnp.where(jnp.arange(2)[:, None, None] == 0, place < group, place > group)
        passed = jnp.sum(jnp.where(wanted, every, 0.0), axis=0)
    pieces = offset(who, scan(who, arrived), passed)
    whole = exchange(pieces, order)

    whole = dict(zip([0] + order, barrier(*(whole[m] for m in [0] + order))))
    whole = [whole[m] for m in range(members)]
    other = swap(relay(range(members), who, near, whole), "core")
    made = outputs(scale, per, part, who, rot, sc, tables, near_other, whole, ())
    made = outputs(scale, per, part, who, rot, sc, tables, None, [other], tuple(made))
    return tuple(made)


def solution(mesh):
    inner, outer = mesh.shape["inner"], mesh.shape["outer"]
    x = inner // 2
    y = x if outer % x == 0 else 1
    z = outer // y
    zl = 2 if z % 2 == 0 else 1
    whole = Mesh(mesh.devices.reshape(x, 2, z // zl, zl, y), ("x", "core", "zh", "zl", "y"))
    rows = ("zh", "zl", "y", "x", "core")
    return jax.shard_map(
        shards,
        mesh=whole,
        in_specs=(P(rows, None),) * 4 + (P(rows),),
        out_specs=(P(rows, None),) * 4,
        check_vma=False,
    )
```

```python
import functools
import itertools
import math

import jax
import jax.numpy as jnp
from jax import lax
from jax.experimental import pallas as pl
from jax.experimental.pallas import tpu as pltpu
from jax.sharding import Mesh, PartitionSpec as P

D = 128
F32 = jnp.float32
BF16 = jnp.bfloat16
VMEM_LIMIT = 20 * 1024 * 1024
HBM = pl.BlockSpec(memory_space=pltpu.HBM)
VMEM = pl.BlockSpec(memory_space=pltpu.VMEM)
SMEM = pl.BlockSpec(memory_space=pltpu.SMEM)


def in_vmem(shape, dtype=F32):
    return pltpu.VMEM(shape, dtype)


def call(body, out_shape, in_specs, out_specs, scratch, flops, moved, name, aliases=None):
    return pl.pallas_call(
        body,
        out_shape=out_shape,
        in_specs=in_specs,
        out_specs=out_specs,
        scratch_shapes=scratch,
        input_output_aliases=aliases or {},
        compiler_params=pltpu.CompilerParams(vmem_limit_bytes=VMEM_LIMIT),
        cost_estimate=pl.CostEstimate(flops=flops, bytes_accessed=moved, transcendentals=0),
        name=name,
    )


def rotate(rows, cosine, sine):
    wide = rows.astype(F32)
    return wide * cosine + pltpu.roll(wide, D // 2, 1) * sine


def unrotate(rows, cosine, sine):
    return rows * cosine - pltpu.roll(rows, D // 2, 1) * sine


def dot(a, b, ca, cb):
    return lax.dot_general(a, b, (((ca,), (cb,)), ((), ())), preferred_element_type=F32)


def rotary_tables(positions):
    rows = positions.shape[1]
    half = D // 2
    lane = lax.broadcasted_iota(jnp.int32, (rows, D), 1)
    index = jnp.where(lane < half, lane, lane - half).astype(F32)
    frequency = jnp.exp(index * (-2.0 * math.log(500000.0) / D))
    place = jnp.broadcast_to(positions.astype(F32), (D, rows)).T
    angle = place * frequency
    sine = jnp.sin(angle)
    return jnp.cos(angle), jnp.where(lane < half, -sine, sine)


def states_body(first, per, sets, _, me, __, core, *refs):
    half, me = core[0], me[0]
    if first:
        pos, *sources = refs[:5]
        cos_ref, sin_ref, *nearby = refs[5:11]
        outs, (place, *inputs), sems = refs[11:13], refs[13:18], refs[18]
        width = inputs[0].shape[1]
        pos_copy = pltpu.make_async_copy(pos, place, sems.at[8])
        pos_copy.start()
        copies = []
        for n, (at, targets) in enumerate(((1 - half, inputs), (half, nearby))):
            start = pl.multiple_of(at * width, width)
            for i, (source, target) in enumerate(zip(sources, targets)):
                copies.append(pltpu.make_async_copy(source.at[:, pl.ds(start, width)], target, sems.at[4 * n + i]))
                copies[-1].start()
        pos_copy.wait()
        cosine, sine = rotary_tables(place[...])
        cos_ref[...] = cosine
        sin_ref[...] = sine
    else:
        cos_ref, sin_ref, *inputs = refs[:6]
        outs = refs[6:]
        cosine, sine = cos_ref[...], sin_ref[...]
    low = me % per
    for side in range(2):
        rows, others = inputs[2 * side : 2 * side + 2]
        if first:
            copies[2 * side].wait()
            copies[2 * side + 1].wait()
        for group, out in zip(sets, outs):
            cut = out.shape[2]
            for n, mask in enumerate(group):
                cols = pl.ds(pl.multiple_of(((me // per) ^ mask) * D, D), D)
                turned = rotate(rows[:, cols], cosine, sine).astype(BF16)
                state = dot(turned, others[:, cols], 0, 0)
                for i in range(per):
                    out[n * per + (low ^ i), side] = state[i * cut : (i + 1) * cut]
    if first:
        for copy in copies[4:]:
            copy.wait()


def states(who, first, per, sets, sources, tables_or_pos):
    rows, width = sources[0].shape
    heads = sum(map(len, sets))
    table = in_vmem((rows, D))
    results = [in_vmem((len(group) * per, 2, D // per, D)) for group in sets]
    body = functools.partial(states_body, first, per, sets)
    work = (4 * heads * rows * D * D, heads * D * (8 * rows + 8 * D))
    if first:
        piece = (rows, heads * D)
        scratch = [pltpu.VMEM((1, rows), jnp.int32)] + [pltpu.VMEM(piece, BF16)] * 4 + [pltpu.SemaphoreType.DMA((9,))]
        out = call(
            body, [table] * 2 + [in_vmem(piece, BF16)] * 4 + results, [SMEM] * 4 + [HBM] * 5, [VMEM] * 8,
            scratch, *work, "block_states",
        )(*who, tables_or_pos, *sources)
        return out[:2], out[2:6], out[6:]
    return call(body, results, [SMEM] * 4 + [VMEM] * 6, [VMEM] * 2, [], *work, "block_states")(
        *who, *tables_or_pos, *sources
    )


def add_body(a_ref, b_ref, *pieces):
    for n, piece in enumerate(pieces):
        piece[...] = a_ref[n] + b_ref[n]


def add(a, b):
    count, _, cut, _ = a.shape
    return call(
        add_body, [in_vmem((2, cut, D))] * count, [VMEM] * 2, [VMEM] * count, [], a.size, a.size * 12, "chip_sum",
    )(a, b)


def total_body(_, __, group, ___, *refs):
    group = group[0]
    out_ref = refs[-1]
    for side in range(2):
        total = refs[0][side]
        for ref in refs[1:-1]:
            total = total + ref[side]
        if out_ref.shape[0] == 2:
            out_ref[side] = total
        elif side == 0:
            keys = total
        else:
            out_ref[0] = jnp.where(group == 0, keys, total)


def total(who, pieces, kinds):
    _, cut, _ = pieces[0].shape
    size = len(pieces) * pieces[0].size
    return call(
        total_body, in_vmem((kinds, cut, D)), [SMEM] * 4 + [VMEM] * len(pieces), VMEM, [], size, size * 4, "block_total",
    )(*who, *pieces)


def offset_body(members, _, __, group, ___, passed_ref, *refs):
    group = group[0]
    for side in range(2):
        if passed_ref.shape[0] == 1:
            extra = jnp.where(group == 1 - side, passed_ref[0], 0.0)
        else:
            extra = passed_ref[side]
        for m in range(members):
            refs[members + m][side] = refs[m][side] + extra


def offset(who, sums, passed):
    members = len(sums)
    size = members * sums[0].size
    return call(
        functools.partial(offset_body, members), [in_vmem(sums[0].shape)] * members,
        [SMEM] * 4 + [VMEM] * (members + 1), [VMEM] * members, [], size, size * 8, "group_sum",
    )(*who, passed, *sums)


def scan_body(members, _, me, __, ___, *refs):
    pieces, sums, (held, ran) = refs[:members], refs[members : 2 * members], refs[2 * members :]
    me = me[0]
    for m in range(members):
        held[me ^ m] = pieces[m][...]
    for side, order in enumerate((range(members), reversed(range(members)))):
        total = jnp.zeros(held.shape[2:], F32)
        for j in order:
            ran[j, side] = total
            total = total + held[j, side]
    for m in range(members):
        sums[m][...] = ran[me ^ m]


def scan(who, pieces):
    members, (_, cut, _) = len(pieces), pieces[0].shape
    shape = (members, 2, cut, D)
    size = math.prod(shape)
    return call(
        functools.partial(scan_body, members), [in_vmem((2, cut, D))] * members,
        [SMEM] * 4 + [VMEM] * members, [VMEM] * members, [pltpu.VMEM(shape, F32)] * 2, size, size * 8, "chip_scan",
    )(*who, *pieces)


def local_body(q_ref, k_ref, v_ref, g_ref, cos_ref, sin_ref, rot_ref, part_ref, sc_ref):
    cosine, sine = cos_ref[...], sin_ref[...]
    rows = q_ref.shape[0]
    row = lax.broadcasted_iota(jnp.int32, (rows, rows), 0)
    col = lax.broadcasted_iota(jnp.int32, (rows, rows), 1)

    def scores(a, b, kept):
        return jnp.where(kept, dot(a, b, 1, 1), 0.0).astype(BF16)

    for h in range(rot_ref.shape[0]):
        cols = slice(h * D, (h + 1) * D)
        krot = rotate(k_ref[:, cols], cosine, sine).astype(BF16)
        qrot = rotate(q_ref[:, cols], cosine, sine).astype(BF16)
        v, g = v_ref[:, cols], g_ref[:, cols]
        for i, value in enumerate((qrot, g, v, krot)):
            rot_ref[h, i] = value
        sc_ref[h, 0] = scores(qrot, krot, row >= col)
        sc_ref[h, 1] = scores(g, v, row >= col)
        sc_ref[h, 2] = scores(v, g, row <= col)
        sc_ref[h, 3] = scores(krot, qrot, row <= col)
    for h in range(rot_ref.shape[0]):
        for i, other in enumerate((2, 3, 0, 1)):
            part_ref[h, i] = dot(sc_ref[h, i], rot_ref[h, other], 1, 0)


def local_parts(q, k, v, g, cosine, sine, heads):
    rows = q.shape[0]
    return call(
        local_body,
        [in_vmem((heads, 4, rows, D), BF16), in_vmem((heads, 4, rows, D))],
        [VMEM] * 6, [VMEM] * 2, [pltpu.VMEM((heads, 4, rows, rows), BF16)], 16 * heads * rows * D * D, 16 * rows * heads * D * 2, "local_parts",
    )(q, k, v, g, cosine, sine)


def outputs_body(scale, per, heads, far, spots, core, me, _, __, rot_ref, part_ref, cos_ref, sin_ref, *refs):
    core, me = core[0], me[0]
    count = heads * per
    if far:
        pieces, refs = refs[:1], refs[5:]
    else:
        extras, pieces, refs = refs[:2], refs[2 : 2 + count], refs[2 + count :]
    outs, (state_ref, held, sems) = refs[:4], refs[4:]
    cosine, sine = cos_ref[...], sin_ref[...]
    copies = []
    for n in range(heads):
        low = me % per
        head = (me // per) ^ n
        for i in range(per):
            cut = pieces[0].shape[-2]
            at = pl.ds(pl.multiple_of((low ^ i) * cut, cut), cut)
            for side in range(2):
                if far:
                    state = pieces[0][n * per + i, side]
                else:
                    which, spot = spots[n]
                    extra = extras[which][spot * per + i, side]
                    state = pieces[n * per + i][side] + jnp.where(core == 1 - side, extra, 0.0)
                state_ref[n, side, at] = state.astype(BF16)
        before, after = state_ref[n, 0], state_ref[n, 1]
        at = (1 - core if far else core) * heads + head
        att = part_ref[at, 0] + dot(rot_ref[at, 0], before, 1, 0)
        rqg = part_ref[at, 1] + dot(rot_ref[at, 1], before, 1, 1)
        rkg = part_ref[at, 2] + dot(rot_ref[at, 2], after, 1, 1)
        vg = part_ref[at, 3] + dot(rot_ref[at, 3], after, 1, 0)
        held[n, 0] = (scale * att).astype(BF16)
        held[n, 1] = unrotate(scale * rqg, cosine, sine).astype(BF16)
        held[n, 2] = unrotate(scale * rkg, cosine, sine).astype(BF16)
        held[n, 3] = (scale * vg).astype(BF16)
        for i in range(4):
            cols = pl.ds(pl.multiple_of(at * D, D), D)
            copies.append(pltpu.make_async_copy(held.at[n, i], outs[i].at[:, cols], sems.at[n, i]))
            copies[-1].start()
    for copy in copies:
        copy.wait()


def outputs(scale, per, count, spots, who, rot, local, tables, extra, pieces, prior):
    heads, _, rows, _ = rot.shape
    far = extra is None
    pieces = list(pieces) if far else [*extra, *pieces]
    return call(
        functools.partial(outputs_body, scale, per, count, far, spots),
        [pltpu.HBM((rows, heads * D), BF16)] * 4,
        [SMEM] * 4 + [VMEM] * (4 + len(pieces)) + [HBM] * len(prior),
        [HBM] * 4,
        [
            pltpu.VMEM((count, 2, D, D), BF16),
            pltpu.VMEM((count, 4, rows, D), BF16),
            pltpu.SemaphoreType.DMA((count, 4)),
        ],
        8 * count * rows * D * D,
        16 * rows * count * D * 2,
        "block_outputs",
        {8 + len(pieces) + i: i for i in range(len(prior))},
    )(*who, rot, local, *tables, *pieces, *prior)


def relay_body(per, spots, core, _, __, ___, near_1, near_2, *refs):
    core = core[0]
    out_ref = refs[-1]
    for m in range(out_ref.shape[0]):
        which, spot = spots[m // per]
        near = (near_1, near_2)[which]
        for side in range(2):
            out_ref[m, side] = refs[m][side] + jnp.where(core == side, near[spot * per + m % per, side], 0.0)


def relay(per, spots, who, near, pieces):
    size = len(pieces) * pieces[0].size
    return call(
        functools.partial(relay_body, per, spots), in_vmem((len(pieces),) + pieces[0].shape),
        [SMEM] * 4 + [VMEM] * (2 + len(pieces)), VMEM, [], size, size * 8, "sibling_state",
    )(*who, *near, *pieces)


def swap(value, axis):
    return lax.ppermute(value, axis, [(0, 1), (1, 0)])


AXES = ("x", "zl", "y")


def send_to(value, mask):
    x, zl, y = (lax.axis_size(axis) for axis in AXES)
    mx, my, mz = mask % x, mask // x % y, mask // (x * y)
    place = lambda a, b, c: (a * zl + b) * y + c
    pairs = [
        (place(a, b, c), place(a ^ mx, b ^ mz, c ^ my))
        for a, b, c in itertools.product(range(x), range(zl), range(y))
    ]
    return lax.ppermute(value, AXES, pairs)


def barrier(*values):
    return lax.optimization_barrier(values)


def exchange(pieces, order):
    arrived = {m: send_to(pieces[m], m) for m in order}
    arrived[0] = pieces[0]
    return arrived


def shards(q, k, v, g, positions):
    rows, width = q.shape
    heads = width // D
    part = heads // 2
    tokens = rows
    for axis in ("x", "core", "zh", "zl", "y"):
        tokens = tokens * lax.axis_size(axis)
    scale = (D * tokens) ** (-0.5)
    core, group = lax.axis_index("core"), lax.axis_index("zh")
    members, groups = lax.axis_size(("zl", "y", "x")), lax.axis_size("zh")
    me = lax.axis_index(("zl", "y", "x"))
    who = [scalar.reshape(1) for scalar in (core, me, group, core)]
    per = members // part
    pos = positions.reshape(1, rows)

    order = []
    for m in sorted(range(1, members - 1), key=lambda m: (bin(m).count("1"), m))[: members // 2 - 1]:
        order += [m, members - 1 - m]
    order.append(members - 1)
    masks = list(dict.fromkeys([m // per for m in order] + [0]))
    sets = masks[: part // 2], masks[part // 2 :]
    spots = {mask: (which, group.index(mask)) for which, group in enumerate(sets) for mask in group}

    sources = [pltpu.with_memory_space_constraint(a, pltpu.HBM) for a in (k, v, q, g)]
    tables, nearby, far = states(who, True, per, sets, sources, pltpu.with_memory_space_constraint(pos, pltpu.HBM))
    near_other = [swap(value, "core") for value in far]
    near = states(who, False, per, sets, nearby, tables)
    summed = [add(*pair) for pair in zip(near, near_other)]
    pieces = {mask * per + i: summed[which][n * per + i] for mask, (which, n) in spots.items() for i in range(per)}
    pieces = [pieces[m] for m in range(members)]
    pieces[order[0]], tables = barrier(pieces[order[0]], tables)
    arrived = exchange(pieces, order)
    rot, local = local_parts(q, k, v, g, *tables, heads)
    listed, rot, local = barrier([arrived[m] for m in order], rot, local)
    arrived = [pieces[0]] + [listed[order.index(m)] for m in range(1, members)]

    send = total(who, arrived, 1 if groups == 2 else 2)
    if groups == 2:
        passed = swap(send, "zh")
    else:
        every = lax.all_gather(send, "zh")
        place = jnp.arange(groups)[:, None, None, None]
        wanted = jnp.where(jnp.arange(2)[:, None, None] == 0, place < group, place > group)
        passed = jnp.sum(jnp.where(wanted, every, 0.0), axis=0)
    pieces = offset(who, scan(who, arrived), passed)
    whole = exchange(pieces, order)

    whole = dict(zip([0] + order, barrier(*(whole[m] for m in [0] + order))))
    whole = [whole[m] for m in range(members)]
    other = swap(relay(per, spots, who, near, whole), "core")
    made = outputs(scale, per, part, spots, who, rot, local, tables, near_other, whole, ())
    made = outputs(scale, per, part, spots, who, rot, local, tables, None, [other], tuple(made))
    return tuple(made)


def solution(mesh):
    inner, outer = mesh.shape["inner"], mesh.shape["outer"]
    x = inner // 2
    y = x if outer % x == 0 else 1
    z = outer // y
    zl = 2 if z % 2 == 0 else 1
    whole = Mesh(mesh.devices.reshape(x, 2, z // zl, zl, y), ("x", "core", "zh", "zl", "y"))
    rows = ("zh", "zl", "y", "x", "core")
    return jax.shard_map(
        shards,
        mesh=whole,
        in_specs=(P(rows, None),) * 4 + (P(rows),),
        out_specs=(P(rows, None),) * 4,
        check_vma=False,
    )
```

```python
import functools
import itertools
import math

import jax
import jax.numpy as jnp
from jax import lax
from jax.experimental import pallas as pl
from jax.experimental.pallas import tpu as pltpu
from jax.sharding import Mesh, PartitionSpec as P

D = 128
F32 = jnp.float32
BF16 = jnp.bfloat16
VMEM_LIMIT = 20 * 1024 * 1024
HBM = pl.BlockSpec(memory_space=pltpu.HBM)
VMEM = pl.BlockSpec(memory_space=pltpu.VMEM)
SMEM = pl.BlockSpec(memory_space=pltpu.SMEM)


def in_vmem(shape, dtype=F32):
    return pltpu.VMEM(shape, dtype)


def call(body, out_shape, in_specs, out_specs, scratch, flops, moved, name, aliases=None):
    return pl.pallas_call(
        body,
        out_shape=out_shape,
        in_specs=in_specs,
        out_specs=out_specs,
        scratch_shapes=scratch,
        input_output_aliases=aliases or {},
        compiler_params=pltpu.CompilerParams(vmem_limit_bytes=VMEM_LIMIT),
        cost_estimate=pl.CostEstimate(flops=flops, bytes_accessed=moved, transcendentals=0),
        name=name,
    )


def rotate(rows, cosine, sine):
    wide = rows.astype(F32)
    return wide * cosine + pltpu.roll(wide, D // 2, 1) * sine


def unrotate(rows, cosine, sine):
    return rows * cosine - pltpu.roll(rows, D // 2, 1) * sine


def dot(a, b, ca, cb):
    return lax.dot_general(a, b, (((ca,), (cb,)), ((), ())), preferred_element_type=F32)


def rotary_tables(positions):
    rows = positions.shape[1]
    half = D // 2
    lane = lax.broadcasted_iota(jnp.int32, (rows, D), 1)
    index = jnp.where(lane < half, lane, lane - half).astype(F32)
    frequency = jnp.exp(index * (-2.0 * math.log(500000.0) / D))
    place = jnp.broadcast_to(positions.astype(F32), (D, rows)).T
    angle = place * frequency
    sine = jnp.sin(angle)
    return jnp.cos(angle), jnp.where(lane < half, -sine, sine)


def states_body(first, per, sets, _, me, __, core, *refs):
    half, me = core[0], me[0]
    if first:
        pos, *sources = refs[:5]
        cos_ref, sin_ref, *nearby = refs[5:11]
        outs, (place, *inputs), sems = refs[11:13], refs[13:18], refs[18]
        width = inputs[0].shape[1]
        pos_copy = pltpu.make_async_copy(pos, place, sems.at[8])
        pos_copy.start()
        copies = []
        for n, (at, targets) in enumerate(((1 - half, inputs), (half, nearby))):
            start = pl.multiple_of(at * width, width)
            for i, (source, target) in enumerate(zip(sources, targets)):
                copies.append(pltpu.make_async_copy(source.at[:, pl.ds(start, width)], target, sems.at[4 * n + i]))
                copies[-1].start()
        pos_copy.wait()
        cosine, sine = rotary_tables(place[...])
        cos_ref[...] = cosine
        sin_ref[...] = sine
    else:
        cos_ref, sin_ref, *inputs = refs[:6]
        outs = refs[6:]
        cosine, sine = cos_ref[...], sin_ref[...]
    low = me % per
    for side in range(2):
        rows, others = inputs[2 * side : 2 * side + 2]
        if first:
            copies[2 * side].wait()
            copies[2 * side + 1].wait()
        for group, out in zip(sets, outs):
            cut = out.shape[2]
            for n, mask in enumerate(group):
                cols = pl.ds(pl.multiple_of(((me // per) ^ mask) * D, D), D)
                turned = rotate(rows[:, cols], cosine, sine).astype(BF16)
                state = dot(turned, others[:, cols], 0, 0)
                for i in range(per):
                    out[n * per + (low ^ i), side] = state[i * cut : (i + 1) * cut]
    if first:
        for copy in copies[4:]:
            copy.wait()


def states(who, first, per, sets, sources, tables_or_pos):
    rows, width = sources[0].shape
    heads = sum(map(len, sets))
    table = in_vmem((rows, D))
    results = [in_vmem((len(group) * per, 2, D // per, D)) for group in sets]
    body = functools.partial(states_body, first, per, sets)
    work = (4 * heads * rows * D * D, heads * D * (8 * rows + 8 * D))
    if first:
        piece = (rows, heads * D)
        scratch = [pltpu.VMEM((1, rows), jnp.int32)] + [pltpu.VMEM(piece, BF16)] * 4 + [pltpu.SemaphoreType.DMA((9,))]
        out = call(
            body, [table] * 2 + [in_vmem(piece, BF16)] * 4 + results, [SMEM] * 4 + [HBM] * 5, [VMEM] * 8,
            scratch, *work, "block_states",
        )(*who, tables_or_pos, *sources)
        return out[:2], out[2:6], out[6:]
    return call(body, results, [SMEM] * 4 + [VMEM] * 6, [VMEM] * 2, [], *work, "block_states")(
        *who, *tables_or_pos, *sources
    )


def add_body(a_ref, b_ref, *pieces):
    for n, piece in enumerate(pieces):
        piece[...] = a_ref[n] + b_ref[n]


def add(a, b):
    count, _, cut, _ = a.shape
    return call(
        add_body, [in_vmem((2, cut, D))] * count, [VMEM] * 2, [VMEM] * count, [], a.size, a.size * 12, "chip_sum",
    )(a, b)


def total_body(_, __, group, ___, *refs):
    group = group[0]
    out_ref = refs[-1]
    for side in range(2):
        total = refs[0][side]
        for ref in refs[1:-1]:
            total = total + ref[side]
        if out_ref.shape[0] == 2:
            out_ref[side] = total
        elif side == 0:
            keys = total
        else:
            out_ref[0] = jnp.where(group == 0, keys, total)


def total(who, pieces, kinds):
    _, cut, _ = pieces[0].shape
    size = len(pieces) * pieces[0].size
    return call(
        total_body, in_vmem((kinds, cut, D)), [SMEM] * 4 + [VMEM] * len(pieces), VMEM, [], size, size * 4, "block_total",
    )(*who, *pieces)


def offset_body(members, _, __, group, ___, passed_ref, *refs):
    group = group[0]
    for side in range(2):
        if passed_ref.shape[0] == 1:
            extra = jnp.where(group == 1 - side, passed_ref[0], 0.0)
        else:
            extra = passed_ref[side]
        for m in range(members):
            refs[members + m][side] = refs[m][side] + extra


def offset(who, sums, passed):
    members = len(sums)
    size = members * sums[0].size
    return call(
        functools.partial(offset_body, members), [in_vmem(sums[0].shape)] * members,
        [SMEM] * 4 + [VMEM] * (members + 1), [VMEM] * members, [], size, size * 8, "group_sum",
    )(*who, passed, *sums)


def scan_body(members, _, me, __, ___, *refs):
    pieces, sums, (held, ran) = refs[:members], refs[members : 2 * members], refs[2 * members :]
    me = me[0]
    for m in range(members):
        held[me ^ m] = pieces[m][...]
    for side, order in enumerate((range(members), reversed(range(members)))):
        total = jnp.zeros(held.shape[2:], F32)
        for j in order:
            ran[j, side] = total
            total = total + held[j, side]
    for m in range(members):
        sums[m][...] = ran[me ^ m]


def scan(who, pieces):
    members, (_, cut, _) = len(pieces), pieces[0].shape
    shape = (members, 2, cut, D)
    size = math.prod(shape)
    return call(
        functools.partial(scan_body, members), [in_vmem((2, cut, D))] * members,
        [SMEM] * 4 + [VMEM] * members, [VMEM] * members, [pltpu.VMEM(shape, F32)] * 2, size, size * 8, "chip_scan",
    )(*who, *pieces)


def local_body(q_ref, k_ref, v_ref, g_ref, cos_ref, sin_ref, rot_ref, part_ref, sc_ref):
    cosine, sine = cos_ref[...], sin_ref[...]
    rows = q_ref.shape[0]
    row = lax.broadcasted_iota(jnp.int32, (rows, rows), 0)
    col = lax.broadcasted_iota(jnp.int32, (rows, rows), 1)

    def scores(a, b, kept):
        return jnp.where(kept, dot(a, b, 1, 1), 0.0).astype(BF16)

    for h in range(rot_ref.shape[0]):
        cols = slice(h * D, (h + 1) * D)
        krot = rotate(k_ref[:, cols], cosine, sine).astype(BF16)
        qrot = rotate(q_ref[:, cols], cosine, sine).astype(BF16)
        v, g = v_ref[:, cols], g_ref[:, cols]
        for i, value in enumerate((qrot, g, v, krot)):
            rot_ref[h, i] = value
        sc_ref[h, 0] = scores(qrot, krot, row >= col)
        sc_ref[h, 1] = scores(g, v, row >= col)
        sc_ref[h, 2] = scores(v, g, row <= col)
        sc_ref[h, 3] = scores(krot, qrot, row <= col)
    for h in range(rot_ref.shape[0]):
        for i, other in enumerate((2, 3, 0, 1)):
            part_ref[h, i] = dot(sc_ref[h, i], rot_ref[h, other], 1, 0)


def local_parts(q, k, v, g, cosine, sine, heads):
    rows = q.shape[0]
    return call(
        local_body,
        [in_vmem((heads, 4, rows, D), BF16), in_vmem((heads, 4, rows, D))],
        [VMEM] * 6, [VMEM] * 2, [pltpu.VMEM((heads, 4, rows, rows), BF16)], 16 * heads * rows * D * D, 16 * rows * heads * D * 2, "local_parts",
    )(q, k, v, g, cosine, sine)


def outputs_body(scale, per, jobs, arrays, prior, spots, core, me, _, __, rot_ref, part_ref, cos_ref, sin_ref, *refs):
    core, me = core[0], me[0]
    extras, pieces, refs = refs[:2], refs[2 : 2 + arrays], refs[2 + arrays + prior :]
    outs, (state_ref, held, sems) = refs[:4], refs[4:]
    cosine, sine = cos_ref[...], sin_ref[...]
    half = rot_ref.shape[0] // 2
    copies = []
    for n, (mask, mine, first, spot) in enumerate(jobs):
        low = me % per
        head = (me // per) ^ mask
        for i in range(per):
            cut = pieces[0].shape[-2]
            at = pl.ds(pl.multiple_of((low ^ i) * cut, cut), cut)
            for side in range(2):
                if mine:
                    which, kept = spots[mask]
                    extra = extras[which][kept * per + i, side]
                    state = pieces[first + i][side] + jnp.where(core == 1 - side, extra, 0.0)
                else:
                    state = pieces[first][spot * per + i, side]
                state_ref[n, side, at] = state.astype(BF16)
        before, after = state_ref[n, 0], state_ref[n, 1]
        at = (core if mine else 1 - core) * half + head
        att = part_ref[at, 0] + dot(rot_ref[at, 0], before, 1, 0)
        rqg = part_ref[at, 1] + dot(rot_ref[at, 1], before, 1, 1)
        rkg = part_ref[at, 2] + dot(rot_ref[at, 2], after, 1, 1)
        vg = part_ref[at, 3] + dot(rot_ref[at, 3], after, 1, 0)
        held[n, 0] = (scale * att).astype(BF16)
        held[n, 1] = unrotate(scale * rqg, cosine, sine).astype(BF16)
        held[n, 2] = unrotate(scale * rkg, cosine, sine).astype(BF16)
        held[n, 3] = (scale * vg).astype(BF16)
        for i in range(4):
            cols = pl.ds(pl.multiple_of(at * D, D), D)
            copies.append(pltpu.make_async_copy(held.at[n, i], outs[i].at[:, cols], sems.at[n, i]))
            copies[-1].start()
    for copy in copies:
        copy.wait()


def outputs(scale, per, spots, who, rot, local, tables, kept, own, far, prior):
    heads, _, rows, _ = rot.shape
    jobs, pieces = [], []
    for mask, values in own:
        jobs.append((mask, True, len(pieces), 0))
        pieces += values
    for masks, value in far:
        jobs += [(mask, False, len(pieces), spot) for spot, mask in enumerate(masks)]
        pieces.append(value)
    count = len(jobs)
    return call(
        functools.partial(outputs_body, scale, per, jobs, len(pieces), len(prior), spots),
        [pltpu.HBM((rows, heads * D), BF16)] * 4,
        [SMEM] * 4 + [VMEM] * (6 + len(pieces)) + [HBM] * len(prior),
        [HBM] * 4,
        [
            pltpu.VMEM((count, 2, D, D), BF16),
            pltpu.VMEM((count, 4, rows, D), BF16),
            pltpu.SemaphoreType.DMA((count, 4)),
        ],
        8 * count * rows * D * D,
        16 * rows * count * D * 2,
        "block_outputs",
        {10 + len(pieces) + i: i for i in range(len(prior))},
    )(*who, rot, local, *tables, *kept, *pieces, *prior)


def relay_body(per, masks, spots, core, _, __, ___, near_1, near_2, *refs):
    core = core[0]
    out_ref = refs[-1]
    for n, mask in enumerate(masks):
        which, spot = spots[mask]
        near = (near_1, near_2)[which]
        for i in range(per):
            for side in range(2):
                extra = jnp.where(core == side, near[spot * per + i, side], 0.0)
                out_ref[n * per + i, side] = refs[n * per + i][side] + extra


def relay(per, masks, spots, who, near, pieces):
    size = len(pieces) * pieces[0].size
    return call(
        functools.partial(relay_body, per, masks, spots), in_vmem((len(pieces),) + pieces[0].shape),
        [SMEM] * 4 + [VMEM] * (2 + len(pieces)), VMEM, [], size, size * 8, "sibling_state",
    )(*who, *near, *pieces)


def swap(value, axis):
    return lax.ppermute(value, axis, [(0, 1), (1, 0)])


AXES = ("x", "zl", "y")


def send_to(value, mask):
    x, zl, y = (lax.axis_size(axis) for axis in AXES)
    mx, my, mz = mask % x, mask // x % y, mask // (x * y)
    place = lambda a, b, c: (a * zl + b) * y + c
    pairs = [
        (place(a, b, c), place(a ^ mx, b ^ mz, c ^ my))
        for a, b, c in itertools.product(range(x), range(zl), range(y))
    ]
    return lax.ppermute(value, AXES, pairs)


def barrier(*values):
    return lax.optimization_barrier(values)


def exchange(pieces, order):
    arrived = {m: send_to(pieces[m], m) for m in order}
    arrived[0] = pieces[0]
    return arrived


def shards(q, k, v, g, positions):
    rows, width = q.shape
    heads = width // D
    part = heads // 2
    tokens = rows
    for axis in ("x", "core", "zh", "zl", "y"):
        tokens = tokens * lax.axis_size(axis)
    scale = (D * tokens) ** (-0.5)
    core, group = lax.axis_index("core"), lax.axis_index("zh")
    members, groups = lax.axis_size(("zl", "y", "x")), lax.axis_size("zh")
    me = lax.axis_index(("zl", "y", "x"))
    who = [scalar.reshape(1) for scalar in (core, me, group, core)]
    per = members // part
    pos = positions.reshape(1, rows)

    order = []
    for m in sorted(range(1, members - 1), key=lambda m: (bin(m).count("1"), m))[: members // 2 - 1]:
        order += [m, members - 1 - m]
    order.append(members - 1)
    masks = list(dict.fromkeys([m // per for m in order] + [0]))
    sets = masks[: part // 2], masks[part // 2 :]
    spots = {mask: (which, group.index(mask)) for which, group in enumerate(sets) for mask in group}

    sources = [pltpu.with_memory_space_constraint(a, pltpu.HBM) for a in (k, v, q, g)]
    tables, nearby, far = states(who, True, per, sets, sources, pltpu.with_memory_space_constraint(pos, pltpu.HBM))
    near_other = [swap(value, "core") for value in far]
    near = states(who, False, per, sets, nearby, tables)
    summed = [add(*pair) for pair in zip(near, near_other)]
    pieces = {mask * per + i: summed[which][n * per + i] for mask, (which, n) in spots.items() for i in range(per)}
    pieces = [pieces[m] for m in range(members)]
    pieces[order[0]], tables = barrier(pieces[order[0]], tables)
    arrived = exchange(pieces, order)
    rot, local = local_parts(q, k, v, g, *tables, heads)
    listed, rot, local = barrier([arrived[m] for m in order], rot, local)
    arrived = [pieces[0]] + [listed[order.index(m)] for m in range(1, members)]

    send = total(who, arrived, 1 if groups == 2 else 2)
    if groups == 2:
        passed = swap(send, "zh")
    else:
        every = lax.all_gather(send, "zh")
        place = jnp.arange(groups)[:, None, None, None]
        wanted = jnp.where(jnp.arange(2)[:, None, None] == 0, place < group, place > group)
        passed = jnp.sum(jnp.where(wanted, every, 0.0), axis=0)
    pieces = offset(who, scan(who, arrived), passed)
    whole = exchange(pieces, order)

    whole = {mask: [whole[mask * per + i] for i in range(per)] for mask in masks}

    def pass_on(chosen):
        listed = [piece for mask in chosen for piece in whole[mask]]
        return chosen, swap(relay(per, chosen, spots, who, near, listed), "core")

    early, late = masks[: part // 2], masks[part // 2 :]
    soon = list(dict.fromkeys([0, *early]))
    first = [pass_on([mask]) for mask in early]
    finish = functools.partial(outputs, scale, per, spots, who, rot, local, tables, near_other)
    made = finish([(mask, whole[mask]) for mask in soon], [], ())
    held = [whole[mask] for mask in late]
    held, first, made = barrier(held, [value for _, value in first], made)
    whole.update(zip(late, held))
    first = [([mask], value) for mask, value in zip(early, first)]
    last = pass_on(late)
    made = finish([(mask, whole[mask]) for mask in late if mask not in soon], first, tuple(made))
    return tuple(finish([], [last], tuple(made)))


def solution(mesh):
    inner, outer = mesh.shape["inner"], mesh.shape["outer"]
    x = inner // 2
    y = x if outer % x == 0 else 1
    z = outer // y
    zl = 2 if z % 2 == 0 else 1
    whole = Mesh(mesh.devices.reshape(x, 2, z // zl, zl, y), ("x", "core", "zh", "zl", "y"))
    rows = ("zh", "zl", "y", "x", "core")
    return jax.shard_map(
        shards,
        mesh=whole,
        in_specs=(P(rows, None),) * 4 + (P(rows),),
        out_specs=(P(rows, None),) * 4,
        check_vma=False,
    )
```

```python
import functools
import itertools
import math

import jax
import jax.numpy as jnp
from jax import lax
from jax.experimental import pallas as pl
from jax.experimental.pallas import tpu as pltpu
from jax.sharding import Mesh, PartitionSpec as P

D = 128
F32 = jnp.float32
BF16 = jnp.bfloat16
VMEM_LIMIT = 20 * 1024 * 1024
HBM = pl.BlockSpec(memory_space=pltpu.HBM)
VMEM = pl.BlockSpec(memory_space=pltpu.VMEM)
SMEM = pl.BlockSpec(memory_space=pltpu.SMEM)


def in_vmem(shape, dtype=F32):
    return pltpu.VMEM(shape, dtype)


def call(body, out_shape, in_specs, out_specs, scratch, flops, moved, name, aliases=None):
    return pl.pallas_call(
        body,
        out_shape=out_shape,
        in_specs=in_specs,
        out_specs=out_specs,
        scratch_shapes=scratch,
        input_output_aliases=aliases or {},
        compiler_params=pltpu.CompilerParams(vmem_limit_bytes=VMEM_LIMIT),
        cost_estimate=pl.CostEstimate(flops=flops, bytes_accessed=moved, transcendentals=0),
        name=name,
    )


def rotate(rows, cosine, sine):
    wide = rows.astype(F32)
    return wide * cosine + pltpu.roll(wide, D // 2, 1) * sine


def unrotate(rows, cosine, sine):
    return rows * cosine - pltpu.roll(rows, D // 2, 1) * sine


def dot(a, b, ca, cb):
    return lax.dot_general(a, b, (((ca,), (cb,)), ((), ())), preferred_element_type=F32)


def rotary_tables(positions):
    rows = positions.shape[1]
    half = D // 2
    lane = lax.broadcasted_iota(jnp.int32, (rows, D), 1)
    index = jnp.where(lane < half, lane, lane - half).astype(F32)
    frequency = jnp.exp(index * (-2.0 * math.log(500000.0) / D))
    place = jnp.broadcast_to(positions.astype(F32), (D, rows)).T
    angle = place * frequency
    sine = jnp.sin(angle)
    return jnp.cos(angle), jnp.where(lane < half, -sine, sine)


def states_body(first, per, sets, _, me, __, core, *refs):
    half, me = core[0], me[0]
    if first:
        pos, *sources = refs[:5]
        cos_ref, sin_ref, *fetched = refs[5:15]
        inputs, nearby = fetched[:4], fetched[4:]
        outs, place, sems = refs[15:17], refs[17], refs[18]
        width = inputs[0].shape[1]
        pos_copy = pltpu.make_async_copy(pos, place, sems.at[8])
        pos_copy.start()
        copies = []
        for n, (at, targets) in enumerate(((1 - half, inputs), (half, nearby))):
            start = pl.multiple_of(at * width, width)
            for i, (source, target) in enumerate(zip(sources, targets)):
                copies.append(pltpu.make_async_copy(source.at[:, pl.ds(start, width)], target, sems.at[4 * n + i]))
                copies[-1].start()
        pos_copy.wait()
        cosine, sine = rotary_tables(place[...])
        cos_ref[...] = cosine
        sin_ref[...] = sine
    else:
        cos_ref, sin_ref, *inputs = refs[:6]
        outs = refs[6:]
        cosine, sine = cos_ref[...], sin_ref[...]
    low = me % per
    for side in range(2):
        rows, others = inputs[2 * side : 2 * side + 2]
        if first:
            copies[2 * side].wait()
            copies[2 * side + 1].wait()
        for group, out in zip(sets, outs):
            cut = out.shape[2]
            for n, mask in enumerate(group):
                cols = pl.ds(pl.multiple_of(((me // per) ^ mask) * D, D), D)
                turned = rotate(rows[:, cols], cosine, sine).astype(BF16)
                state = dot(turned, others[:, cols], 0, 0)
                for i in range(per):
                    out[n * per + (low ^ i), side] = state[i * cut : (i + 1) * cut]
    if first:
        for copy in copies[4:]:
            copy.wait()


def states(who, first, per, sets, sources, tables_or_pos):
    rows, width = sources[0].shape
    heads = sum(map(len, sets))
    table = in_vmem((rows, D))
    results = [in_vmem((len(group) * per, 2, D // per, D)) for group in sets]
    body = functools.partial(states_body, first, per, sets)
    work = (4 * heads * rows * D * D, heads * D * (8 * rows + 8 * D))
    if first:
        piece = (rows, heads * D)
        scratch = [pltpu.VMEM((1, rows), jnp.int32), pltpu.SemaphoreType.DMA((9,))]
        out = call(
            body, [table] * 2 + [in_vmem(piece, BF16)] * 8 + results, [SMEM] * 4 + [HBM] * 5, [VMEM] * 12,
            scratch, *work, "block_states",
        )(*who, tables_or_pos, *sources)
        return out[:2], out[2:6], out[6:10], out[10:]
    return call(body, results, [SMEM] * 4 + [VMEM] * 6, [VMEM] * 2, [], *work, "block_states")(
        *who, *tables_or_pos, *sources
    )


def add_body(a_ref, b_ref, *pieces):
    for n, piece in enumerate(pieces):
        piece[...] = a_ref[n] + b_ref[n]


def add(a, b):
    count, _, cut, _ = a.shape
    return call(
        add_body, [in_vmem((2, cut, D))] * count, [VMEM] * 2, [VMEM] * count, [], a.size, a.size * 12, "chip_sum",
    )(a, b)


def total_body(_, __, group, ___, *refs):
    group = group[0]
    out_ref = refs[-1]
    for side in range(2):
        total = refs[0][side]
        for ref in refs[1:-1]:
            total = total + ref[side]
        if out_ref.shape[0] == 2:
            out_ref[side] = total
        elif side == 0:
            keys = total
        else:
            out_ref[0] = jnp.where(group == 0, keys, total)


def total(who, pieces, kinds):
    _, cut, _ = pieces[0].shape
    size = len(pieces) * pieces[0].size
    return call(
        total_body, in_vmem((kinds, cut, D)), [SMEM] * 4 + [VMEM] * len(pieces), VMEM, [], size, size * 4, "block_total",
    )(*who, *pieces)


def offset_body(members, _, __, group, ___, passed_ref, *refs):
    group = group[0]
    for side in range(2):
        if passed_ref.shape[0] == 1:
            extra = jnp.where(group == 1 - side, passed_ref[0], 0.0)
        else:
            extra = passed_ref[side]
        for m in range(members):
            refs[members + m][side] = refs[m][side] + extra


def offset(who, sums, passed):
    members = len(sums)
    size = members * sums[0].size
    return call(
        functools.partial(offset_body, members), [in_vmem(sums[0].shape)] * members,
        [SMEM] * 4 + [VMEM] * (members + 1), [VMEM] * members, [], size, size * 8, "group_sum",
    )(*who, passed, *sums)


def scan_body(members, _, me, __, ___, *refs):
    pieces, sums, (held, ran) = refs[:members], refs[members : 2 * members], refs[2 * members :]
    me = me[0]
    for m in range(members):
        held[me ^ m] = pieces[m][...]
    for side, order in enumerate((range(members), reversed(range(members)))):
        total = jnp.zeros(held.shape[2:], F32)
        for j in order:
            ran[j, side] = total
            total = total + held[j, side]
    for m in range(members):
        sums[m][...] = ran[me ^ m]


def scan(who, pieces):
    members, (_, cut, _) = len(pieces), pieces[0].shape
    shape = (members, 2, cut, D)
    size = math.prod(shape)
    return call(
        functools.partial(scan_body, members), [in_vmem((2, cut, D))] * members,
        [SMEM] * 4 + [VMEM] * members, [VMEM] * members, [pltpu.VMEM(shape, F32)] * 2, size, size * 8, "chip_scan",
    )(*who, *pieces)


def local_body(*refs):
    halves, (cos_ref, sin_ref, rot_ref, part_ref, sc_ref) = (refs[:4], refs[4:8]), refs[8:]
    cosine, sine = cos_ref[...], sin_ref[...]
    rows = cosine.shape[0]
    row = lax.broadcasted_iota(jnp.int32, (rows, rows), 0)
    col = lax.broadcasted_iota(jnp.int32, (rows, rows), 1)
    heads = rot_ref.shape[0]

    def scores(a, b, kept):
        return jnp.where(kept, dot(a, b, 1, 1), 0.0).astype(BF16)

    for h in range(heads):
        k_ref, v_ref, q_ref, g_ref = halves[h // (heads // 2)]
        cols = slice(h % (heads // 2) * D, (h % (heads // 2) + 1) * D)
        krot = rotate(k_ref[:, cols], cosine, sine).astype(BF16)
        qrot = rotate(q_ref[:, cols], cosine, sine).astype(BF16)
        v, g = v_ref[:, cols], g_ref[:, cols]
        for i, value in enumerate((qrot, g, v, krot)):
            rot_ref[h, i] = value
        sc_ref[h, 0] = scores(qrot, krot, row >= col)
        sc_ref[h, 1] = scores(g, v, row >= col)
        sc_ref[h, 2] = scores(v, g, row <= col)
        sc_ref[h, 3] = scores(krot, qrot, row <= col)
    for h in range(heads):
        for i, other in enumerate((2, 3, 0, 1)):
            part_ref[h, i] = dot(sc_ref[h, i], rot_ref[h, other], 1, 0)


def local_parts(near, far, tables, heads):
    rows = near[0].shape[0]
    return call(
        local_body,
        [in_vmem((heads, 4, rows, D), BF16), in_vmem((heads, 4, rows, D))],
        [VMEM] * 10, [VMEM] * 2, [pltpu.VMEM((heads, 4, rows, rows), BF16)], 16 * heads * rows * D * D,
        16 * rows * heads * D * 2, "local_parts",
    )(*near, *far, *tables)


def outputs_body(scale, per, jobs, arrays, prior, spots, core, me, _, __, rot_ref, part_ref, cos_ref, sin_ref, *refs):
    core, me = core[0], me[0]
    extras, pieces, refs = refs[:2], refs[2 : 2 + arrays], refs[2 + arrays + prior :]
    outs, (state_ref, held, sems) = refs[:4], refs[4:]
    cosine, sine = cos_ref[...], sin_ref[...]
    half = rot_ref.shape[0] // 2
    copies = []
    for n, (mask, mine, first, spot) in enumerate(jobs):
        low = me % per
        head = (me // per) ^ mask
        for i in range(per):
            cut = pieces[0].shape[-2]
            at = pl.ds(pl.multiple_of((low ^ i) * cut, cut), cut)
            for side in range(2):
                if mine:
                    which, kept = spots[mask]
                    extra = extras[which][kept * per + i, side]
                    state = pieces[first + i][side] + jnp.where(core == 1 - side, extra, 0.0)
                else:
                    state = pieces[first][spot * per + i, side]
                state_ref[n, side, at] = state.astype(BF16)
        before, after = state_ref[n, 0], state_ref[n, 1]
        at = head if mine else half + head
        att = part_ref[at, 0] + dot(rot_ref[at, 0], before, 1, 0)
        rqg = part_ref[at, 1] + dot(rot_ref[at, 1], before, 1, 1)
        rkg = part_ref[at, 2] + dot(rot_ref[at, 2], after, 1, 1)
        vg = part_ref[at, 3] + dot(rot_ref[at, 3], after, 1, 0)
        held[n, 0] = (scale * att).astype(BF16)
        held[n, 1] = unrotate(scale * rqg, cosine, sine).astype(BF16)
        held[n, 2] = unrotate(scale * rkg, cosine, sine).astype(BF16)
        held[n, 3] = (scale * vg).astype(BF16)
        column = ((core if mine else 1 - core) * half + head) * D
        for i in range(4):
            cols = pl.ds(pl.multiple_of(column, D), D)
            copies.append(pltpu.make_async_copy(held.at[n, i], outs[i].at[:, cols], sems.at[n, i]))
            copies[-1].start()
    for copy in copies:
        copy.wait()


def outputs(scale, per, spots, who, rot, local, tables, kept, own, far, prior):
    heads, _, rows, _ = rot.shape
    jobs, pieces = [], []
    for mask, values in own:
        jobs.append((mask, True, len(pieces), 0))
        pieces += values
    for masks, value in far:
        jobs += [(mask, False, len(pieces), spot) for spot, mask in enumerate(masks)]
        pieces.append(value)
    count = len(jobs)
    return call(
        functools.partial(outputs_body, scale, per, jobs, len(pieces), len(prior), spots),
        [pltpu.HBM((rows, heads * D), BF16)] * 4,
        [SMEM] * 4 + [VMEM] * (6 + len(pieces)) + [HBM] * len(prior),
        [HBM] * 4,
        [
            pltpu.VMEM((count, 2, D, D), BF16),
            pltpu.VMEM((count, 4, rows, D), BF16),
            pltpu.SemaphoreType.DMA((count, 4)),
        ],
        8 * count * rows * D * D,
        16 * rows * count * D * 2,
        "block_outputs",
        {10 + len(pieces) + i: i for i in range(len(prior))},
    )(*who, rot, local, *tables, *kept, *pieces, *prior)


def relay_body(per, masks, spots, core, _, __, ___, near_1, near_2, *refs):
    core = core[0]
    out_ref = refs[-1]
    for n, mask in enumerate(masks):
        which, spot = spots[mask]
        near = (near_1, near_2)[which]
        for i in range(per):
            for side in range(2):
                extra = jnp.where(core == side, near[spot * per + i, side], 0.0)
                out_ref[n * per + i, side] = refs[n * per + i][side] + extra


def relay(per, masks, spots, who, near, pieces):
    size = len(pieces) * pieces[0].size
    return call(
        functools.partial(relay_body, per, masks, spots), in_vmem((len(pieces),) + pieces[0].shape),
        [SMEM] * 4 + [VMEM] * (2 + len(pieces)), VMEM, [], size, size * 8, "sibling_state",
    )(*who, *near, *pieces)


def swap(value, axis):
    return lax.ppermute(value, axis, [(0, 1), (1, 0)])


AXES = ("x", "zl", "y")


def send_to(value, mask):
    x, zl, y = (lax.axis_size(axis) for axis in AXES)
    mx, my, mz = mask % x, mask // x % y, mask // (x * y)
    place = lambda a, b, c: (a * zl + b) * y + c
    pairs = [
        (place(a, b, c), place(a ^ mx, b ^ mz, c ^ my))
        for a, b, c in itertools.product(range(x), range(zl), range(y))
    ]
    return lax.ppermute(value, AXES, pairs)


def barrier(*values):
    return lax.optimization_barrier(values)


def exchange(pieces, order):
    arrived = {m: send_to(pieces[m], m) for m in order}
    arrived[0] = pieces[0]
    return arrived


def shards(q, k, v, g, positions):
    rows, width = q.shape
    heads = width // D
    part = heads // 2
    tokens = rows
    for axis in ("x", "core", "zh", "zl", "y"):
        tokens = tokens * lax.axis_size(axis)
    scale = (D * tokens) ** (-0.5)
    core, group = lax.axis_index("core"), lax.axis_index("zh")
    members, groups = lax.axis_size(("zl", "y", "x")), lax.axis_size("zh")
    me = lax.axis_index(("zl", "y", "x"))
    who = [scalar.reshape(1) for scalar in (core, me, group, core)]
    per = members // part
    pos = positions.reshape(1, rows)

    order = []
    for m in sorted(range(1, members - 1), key=lambda m: (bin(m).count("1"), m))[: members // 2 - 1]:
        order += [m, members - 1 - m]
    order.append(members - 1)
    masks = list(dict.fromkeys([m // per for m in order] + [0]))
    sets = masks[: part // 2], masks[part // 2 :]
    spots = {mask: (which, group.index(mask)) for which, group in enumerate(sets) for mask in group}

    sources = [pltpu.with_memory_space_constraint(a, pltpu.HBM) for a in (k, v, q, g)]
    tables, faraway, nearby, far = states(who, True, per, sets, sources, pltpu.with_memory_space_constraint(pos, pltpu.HBM))
    near = states(who, False, per, sets, nearby, tables)
    held_back, near = barrier(far[1], near)
    near_other = [swap(far[0], "core"), swap(held_back, "core")]
    summed = [add(*pair) for pair in zip(near, near_other)]
    pieces = {mask * per + i: summed[which][n * per + i] for mask, (which, n) in spots.items() for i in range(per)}
    pieces = [pieces[m] for m in range(members)]
    pieces[order[0]], tables = barrier(pieces[order[0]], tables)
    arrived = exchange(pieces, order)
    rot, local = local_parts(nearby, faraway, tables, heads)
    listed, rot, local = barrier([arrived[m] for m in order], rot, local)
    arrived = [pieces[0]] + [listed[order.index(m)] for m in range(1, members)]

    send = total(who, arrived, 1 if groups == 2 else 2)
    if groups == 2:
        passed = swap(send, "zh")
    else:
        every = lax.all_gather(send, "zh")
        place = jnp.arange(groups)[:, None, None, None]
        wanted = jnp.where(jnp.arange(2)[:, None, None] == 0, place < group, place > group)
        passed = jnp.sum(jnp.where(wanted, every, 0.0), axis=0)
    pieces = offset(who, scan(who, arrived), passed)
    whole = exchange(pieces, order)

    whole = {mask: [whole[mask * per + i] for i in range(per)] for mask in masks}

    def pass_on(chosen):
        listed = [piece for mask in chosen for piece in whole[mask]]
        return chosen, swap(relay(per, chosen, spots, who, near, listed), "core")

    early, late = masks[: part // 2], masks[part // 2 :]
    soon = list(dict.fromkeys([0, *early]))
    first = [pass_on([mask]) for mask in early]
    finish = functools.partial(outputs, scale, per, spots, who, rot, local, tables, near_other)
    made = finish([(mask, whole[mask]) for mask in soon], [], ())
    held = [whole[mask] for mask in late]
    held, first, made = barrier(held, [value for _, value in first], made)
    whole.update(zip(late, held))
    first = [([mask], value) for mask, value in zip(early, first)]
    last = pass_on(late)
    made = finish([(mask, whole[mask]) for mask in late if mask not in soon], first, tuple(made))
    return tuple(finish([], [last], tuple(made)))


def solution(mesh):
    inner, outer = mesh.shape["inner"], mesh.shape["outer"]
    x = inner // 2
    y = x if outer % x == 0 else 1
    z = outer // y
    zl = 2 if z % 2 == 0 else 1
    whole = Mesh(mesh.devices.reshape(x, 2, z // zl, zl, y), ("x", "core", "zh", "zl", "y"))
    rows = ("zh", "zl", "y", "x", "core")
    return jax.shard_map(
        shards,
        mesh=whole,
        in_specs=(P(rows, None),) * 4 + (P(rows),),
        out_specs=(P(rows, None),) * 4,
        check_vma=False,
    )
```

```python
import functools
import itertools
import math

import jax
import jax.numpy as jnp
from jax import lax
from jax.experimental import pallas as pl
from jax.experimental.pallas import tpu as pltpu
from jax.sharding import Mesh, PartitionSpec as P

D = 128
F32 = jnp.float32
BF16 = jnp.bfloat16
VMEM_LIMIT = 20 * 1024 * 1024
HBM = pl.BlockSpec(memory_space=pltpu.HBM)
VMEM = pl.BlockSpec(memory_space=pltpu.VMEM)
SMEM = pl.BlockSpec(memory_space=pltpu.SMEM)


def in_vmem(shape, dtype=F32):
    return pltpu.VMEM(shape, dtype)


def call(body, out_shape, in_specs, out_specs, scratch, flops, moved, name, aliases=None):
    return pl.pallas_call(
        body,
        out_shape=out_shape,
        in_specs=in_specs,
        out_specs=out_specs,
        scratch_shapes=scratch,
        input_output_aliases=aliases or {},
        compiler_params=pltpu.CompilerParams(vmem_limit_bytes=VMEM_LIMIT),
        cost_estimate=pl.CostEstimate(flops=flops, bytes_accessed=moved, transcendentals=0),
        name=name,
    )


def rotate(rows, cosine, sine):
    wide = rows.astype(F32)
    return wide * cosine + pltpu.roll(wide, D // 2, 1) * sine


def unrotate(rows, cosine, sine):
    return rows * cosine - pltpu.roll(rows, D // 2, 1) * sine


def dot(a, b, ca, cb):
    return lax.dot_general(a, b, (((ca,), (cb,)), ((), ())), preferred_element_type=F32)


def rotary_tables(positions):
    rows = positions.shape[1]
    half = D // 2
    index = lax.broadcasted_iota(jnp.int32, (half, rows), 0).astype(F32)
    frequency = jnp.exp(index * (-2.0 * math.log(500000.0) / D))
    angle = positions.astype(F32) * frequency
    cosine, sine = jnp.cos(angle), jnp.sin(angle)
    return jnp.concatenate([cosine, cosine], 0).T, jnp.concatenate([-sine, sine], 0).T


def states_body(first, per, sets, _, me, __, core, *refs):
    half, me = core[0], me[0]
    if first:
        pos, *sources = refs[:5]
        cos_ref, sin_ref, *fetched = refs[5:15]
        inputs, nearby = fetched[:4], fetched[4:]
        outs, place, sems = refs[15:17], refs[17], refs[18]
        width = inputs[0].shape[1]
        pos_copy = pltpu.make_async_copy(pos, place, sems.at[8])
        pos_copy.start()
        copies = []
        for n, (at, targets) in enumerate(((1 - half, inputs), (half, nearby))):
            start = pl.multiple_of(at * width, width)
            for i, (source, target) in enumerate(zip(sources, targets)):
                copies.append(pltpu.make_async_copy(source.at[:, pl.ds(start, width)], target, sems.at[4 * n + i]))
                copies[-1].start()
        pos_copy.wait()
        cosine, sine = rotary_tables(place[...])
        cos_ref[...] = cosine
        sin_ref[...] = sine
    else:
        cos_ref, sin_ref, *inputs = refs[:6]
        outs = refs[6:]
        cosine, sine = cos_ref[...], sin_ref[...]
    low = me % per
    for side in range(2):
        rows, others = inputs[2 * side : 2 * side + 2]
        if first:
            copies[2 * side].wait()
            copies[2 * side + 1].wait()
        for group, out in zip(sets, outs):
            cut = out.shape[2]
            for n, mask in enumerate(group):
                cols = pl.ds(pl.multiple_of(((me // per) ^ mask) * D, D), D)
                turned = rotate(rows[:, cols], cosine, sine).astype(BF16)
                state = dot(turned, others[:, cols], 0, 0)
                for i in range(per):
                    out[n * per + (low ^ i), side] = state[i * cut : (i + 1) * cut]
    if first:
        for copy in copies[4:]:
            copy.wait()


def states(who, first, per, sets, sources, tables_or_pos):
    rows, width = sources[0].shape
    heads = sum(map(len, sets))
    table = in_vmem((rows, D))
    results = [in_vmem((len(group) * per, 2, D // per, D)) for group in sets]
    body = functools.partial(states_body, first, per, sets)
    work = (4 * heads * rows * D * D, heads * D * (8 * rows + 8 * D))
    if first:
        piece = (rows, heads * D)
        scratch = [pltpu.VMEM((1, rows), jnp.int32), pltpu.SemaphoreType.DMA((9,))]
        out = call(
            body, [table] * 2 + [in_vmem(piece, BF16)] * 8 + results, [SMEM] * 4 + [HBM] * 5, [VMEM] * 12,
            scratch, *work, "block_states",
        )(*who, tables_or_pos, *sources)
        return out[:2], out[2:6], out[6:10], out[10:]
    return call(body, results, [SMEM] * 4 + [VMEM] * 6, [VMEM] * 2, [], *work, "block_states")(
        *who, *tables_or_pos, *sources
    )


def add_body(a_ref, b_ref, *pieces):
    for n, piece in enumerate(pieces):
        piece[...] = a_ref[n] + b_ref[n]


def add(a, b):
    count, _, cut, _ = a.shape
    return call(
        add_body, [in_vmem((2, cut, D))] * count, [VMEM] * 2, [VMEM] * count, [], a.size, a.size * 12, "chip_sum",
    )(a, b)


def total_body(_, __, group, ___, *refs):
    group = group[0]
    out_ref = refs[-1]
    for side in range(2):
        total = refs[0][side]
        for ref in refs[1:-1]:
            total = total + ref[side]
        if out_ref.shape[0] == 2:
            out_ref[side] = total
        elif side == 0:
            keys = total
        else:
            out_ref[0] = jnp.where(group == 0, keys, total)


def total(who, pieces, kinds):
    _, cut, _ = pieces[0].shape
    size = len(pieces) * pieces[0].size
    return call(
        total_body, in_vmem((kinds, cut, D)), [SMEM] * 4 + [VMEM] * len(pieces), VMEM, [], size, size * 4, "block_total",
    )(*who, *pieces)


def offset_body(members, _, __, group, ___, passed_ref, *refs):
    group = group[0]
    for side in range(2):
        if passed_ref.shape[0] == 1:
            extra = jnp.where(group == 1 - side, passed_ref[0], 0.0)
        else:
            extra = passed_ref[side]
        for m in range(members):
            refs[members + m][side] = refs[m][side] + extra


def offset(who, sums, passed):
    members = len(sums)
    size = members * sums[0].size
    return call(
        functools.partial(offset_body, members), [in_vmem(sums[0].shape)] * members,
        [SMEM] * 4 + [VMEM] * (members + 1), [VMEM] * members, [], size, size * 8, "group_sum",
    )(*who, passed, *sums)


def scan_body(members, _, me, __, ___, *refs):
    pieces, sums, (held, ran) = refs[:members], refs[members : 2 * members], refs[2 * members :]
    me = me[0]
    for m in range(members):
        held[me ^ m] = pieces[m][...]
    for side, order in enumerate((range(members), reversed(range(members)))):
        total = jnp.zeros(held.shape[2:], F32)
        for j in order:
            ran[j, side] = total
            total = total + held[j, side]
    for m in range(members):
        sums[m][...] = ran[me ^ m]


def scan(who, pieces):
    members, (_, cut, _) = len(pieces), pieces[0].shape
    shape = (members, 2, cut, D)
    size = math.prod(shape)
    return call(
        functools.partial(scan_body, members), [in_vmem((2, cut, D))] * members,
        [SMEM] * 4 + [VMEM] * members, [VMEM] * members, [pltpu.VMEM(shape, F32)] * 2, size, size * 8, "chip_scan",
    )(*who, *pieces)


def local_body(*refs):
    halves, (cos_ref, sin_ref, rot_ref, part_ref, sc_ref) = (refs[:4], refs[4:8]), refs[8:]
    cosine, sine = cos_ref[...], sin_ref[...]
    rows = cosine.shape[0]
    row = lax.broadcasted_iota(jnp.int32, (rows, rows), 0)
    col = lax.broadcasted_iota(jnp.int32, (rows, rows), 1)
    heads = rot_ref.shape[0]

    def scores(a, b, kept):
        return jnp.where(kept, dot(a, b, 1, 1), 0.0).astype(BF16)

    for h in range(heads):
        k_ref, v_ref, q_ref, g_ref = halves[h // (heads // 2)]
        cols = slice(h % (heads // 2) * D, (h % (heads // 2) + 1) * D)
        krot = rotate(k_ref[:, cols], cosine, sine).astype(BF16)
        qrot = rotate(q_ref[:, cols], cosine, sine).astype(BF16)
        v, g = v_ref[:, cols], g_ref[:, cols]
        for i, value in enumerate((qrot, g, v, krot)):
            rot_ref[h, i] = value
        sc_ref[h, 0] = scores(qrot, krot, row >= col)
        sc_ref[h, 1] = scores(g, v, row >= col)
        sc_ref[h, 2] = scores(v, g, row <= col)
        sc_ref[h, 3] = scores(krot, qrot, row <= col)
    for h in range(heads):
        for i, other in enumerate((2, 3, 0, 1)):
            part_ref[h, i] = dot(sc_ref[h, i], rot_ref[h, other], 1, 0)


def local_parts(near, far, tables, heads):
    rows = near[0].shape[0]
    return call(
        local_body,
        [in_vmem((heads, 4, rows, D), BF16), in_vmem((heads, 4, rows, D))],
        [VMEM] * 10, [VMEM] * 2, [pltpu.VMEM((heads, 4, rows, rows), BF16)], 16 * heads * rows * D * D,
        16 * rows * heads * D * 2, "local_parts",
    )(*near, *far, *tables)


def outputs_body(scale, per, jobs, arrays, prior, spots, core, me, _, __, rot_ref, part_ref, cos_ref, sin_ref, *refs):
    core, me = core[0], me[0]
    extras, pieces, refs = refs[:2], refs[2 : 2 + arrays], refs[2 + arrays + prior :]
    outs, (state_ref, held, sems) = refs[:4], refs[4:]
    cosine, sine = cos_ref[...], sin_ref[...]
    half = rot_ref.shape[0] // 2
    copies = []
    for n, (mask, mine, first, spot) in enumerate(jobs):
        low = me % per
        head = (me // per) ^ mask
        for i in range(per):
            cut = pieces[0].shape[-2]
            at = pl.ds(pl.multiple_of((low ^ i) * cut, cut), cut)
            for side in range(2):
                if mine:
                    which, kept = spots[mask]
                    extra = extras[which][kept * per + i, side]
                    state = pieces[first + i][side] + jnp.where(core == 1 - side, extra, 0.0)
                else:
                    state = pieces[first][spot * per + i, side]
                state_ref[n, side, at] = state.astype(BF16)
        before, after = state_ref[n, 0], state_ref[n, 1]
        at = head if mine else half + head
        att = part_ref[at, 0] + dot(rot_ref[at, 0], before, 1, 0)
        rqg = part_ref[at, 1] + dot(rot_ref[at, 1], before, 1, 1)
        rkg = part_ref[at, 2] + dot(rot_ref[at, 2], after, 1, 1)
        vg = part_ref[at, 3] + dot(rot_ref[at, 3], after, 1, 0)
        held[n, 0] = (scale * att).astype(BF16)
        held[n, 1] = unrotate(scale * rqg, cosine, sine).astype(BF16)
        held[n, 2] = unrotate(scale * rkg, cosine, sine).astype(BF16)
        held[n, 3] = (scale * vg).astype(BF16)
        column = ((core if mine else 1 - core) * half + head) * D
        for i in range(4):
            cols = pl.ds(pl.multiple_of(column, D), D)
            copies.append(pltpu.make_async_copy(held.at[n, i], outs[i].at[:, cols], sems.at[n, i]))
            copies[-1].start()
    for copy in copies:
        copy.wait()


def outputs(scale, per, spots, who, rot, local, tables, kept, own, far, prior):
    heads, _, rows, _ = rot.shape
    jobs, pieces = [], []
    for mask, values in own:
        jobs.append((mask, True, len(pieces), 0))
        pieces += values
    for masks, value in far:
        jobs += [(mask, False, len(pieces), spot) for spot, mask in enumerate(masks)]
        pieces.append(value)
    count = len(jobs)
    return call(
        functools.partial(outputs_body, scale, per, jobs, len(pieces), len(prior), spots),
        [pltpu.HBM((rows, heads * D), BF16)] * 4,
        [SMEM] * 4 + [VMEM] * (6 + len(pieces)) + [HBM] * len(prior),
        [HBM] * 4,
        [
            pltpu.VMEM((count, 2, D, D), BF16),
            pltpu.VMEM((count, 4, rows, D), BF16),
            pltpu.SemaphoreType.DMA((count, 4)),
        ],
        8 * count * rows * D * D,
        16 * rows * count * D * 2,
        "block_outputs",
        {10 + len(pieces) + i: i for i in range(len(prior))},
    )(*who, rot, local, *tables, *kept, *pieces, *prior)


def relay_body(per, masks, spots, core, _, __, ___, near_1, near_2, *refs):
    core = core[0]
    out_ref = refs[-1]
    for n, mask in enumerate(masks):
        which, spot = spots[mask]
        near = (near_1, near_2)[which]
        for i in range(per):
            for side in range(2):
                extra = jnp.where(core == side, near[spot * per + i, side], 0.0)
                out_ref[n * per + i, side] = refs[n * per + i][side] + extra


def relay(per, masks, spots, who, near, pieces):
    size = len(pieces) * pieces[0].size
    return call(
        functools.partial(relay_body, per, masks, spots), in_vmem((len(pieces),) + pieces[0].shape),
        [SMEM] * 4 + [VMEM] * (2 + len(pieces)), VMEM, [], size, size * 8, "sibling_state",
    )(*who, *near, *pieces)


def swap(value, axis):
    return lax.ppermute(value, axis, [(0, 1), (1, 0)])


AXES = ("x", "zl", "y")


def send_to(value, mask):
    x, zl, y = (lax.axis_size(axis) for axis in AXES)
    mx, my, mz = mask % x, mask // x % y, mask // (x * y)
    place = lambda a, b, c: (a * zl + b) * y + c
    pairs = [
        (place(a, b, c), place(a ^ mx, b ^ mz, c ^ my))
        for a, b, c in itertools.product(range(x), range(zl), range(y))
    ]
    return lax.ppermute(value, AXES, pairs)


def barrier(*values):
    return lax.optimization_barrier(values)


def exchange(pieces, order):
    arrived = {m: send_to(pieces[m], m) for m in order}
    arrived[0] = pieces[0]
    return arrived


def shards(q, k, v, g, positions):
    rows, width = q.shape
    heads = width // D
    part = heads // 2
    tokens = rows
    for axis in ("x", "core", "zh", "zl", "y"):
        tokens = tokens * lax.axis_size(axis)
    scale = (D * tokens) ** (-0.5)
    core, group = lax.axis_index("core"), lax.axis_index("zh")
    members, groups = lax.axis_size(("zl", "y", "x")), lax.axis_size("zh")
    me = lax.axis_index(("zl", "y", "x"))
    who = [scalar.reshape(1) for scalar in (core, me, group, core)]
    per = members // part
    pos = positions.reshape(1, rows)

    short = sorted(range(1, members - 1), key=lambda m: (bin(m).count("1"), m))[: members // 2 - 1]
    order = [route for m in short for route in (m, members - 1 - m)] + [members - 1]
    back = [route for m in short[:1] + short[:0:-1] for route in (m, members - 1 - m)] + [members - 1]
    masks = list(dict.fromkeys([m // per for m in order] + [0]))
    sets = masks[: part // 2], masks[part // 2 :]
    spots = {mask: (which, group.index(mask)) for which, group in enumerate(sets) for mask in group}

    sources = [pltpu.with_memory_space_constraint(a, pltpu.HBM) for a in (k, v, q, g)]
    tables, faraway, nearby, far = states(who, True, per, sets, sources, pltpu.with_memory_space_constraint(pos, pltpu.HBM))
    near = states(who, False, per, sets, nearby, tables)
    held_back, near = barrier(far[1], near)
    near_other = [swap(far[0], "core"), swap(held_back, "core")]
    summed = [add(*pair) for pair in zip(near, near_other)]
    pieces = {mask * per + i: summed[which][n * per + i] for mask, (which, n) in spots.items() for i in range(per)}
    pieces = [pieces[m] for m in range(members)]
    pieces[order[0]], tables = barrier(pieces[order[0]], tables)
    arrived = exchange(pieces, order)
    rot, local = local_parts(nearby, faraway, tables, heads)
    listed, rot, local = barrier([arrived[m] for m in order], rot, local)
    arrived = [pieces[0]] + [listed[order.index(m)] for m in range(1, members)]

    send = total(who, arrived, 1 if groups == 2 else 2)
    if groups == 2:
        passed = swap(send, "zh")
    else:
        every = lax.all_gather(send, "zh")
        place = jnp.arange(groups)[:, None, None, None]
        wanted = jnp.where(jnp.arange(2)[:, None, None] == 0, place < group, place > group)
        passed = jnp.sum(jnp.where(wanted, every, 0.0), axis=0)
    pieces = offset(who, scan(who, arrived), passed)
    whole = exchange(pieces, back)

    whole = {mask: [whole[mask * per + i] for i in range(per)] for mask in masks}

    def pass_on(chosen):
        listed = [piece for mask in chosen for piece in whole[mask]]
        return chosen, swap(relay(per, chosen, spots, who, near, listed), "core")

    returned = list(dict.fromkeys([m // per for m in back] + [0]))
    early, late = returned[: part // 2], returned[part // 2 :]
    soon = list(dict.fromkeys([0, *early]))
    first = [pass_on([mask]) for mask in early]
    finish = functools.partial(outputs, scale, per, spots, who, rot, local, tables, near_other)
    made = finish([(mask, whole[mask]) for mask in soon], [], ())
    held = [whole[mask] for mask in late]
    held, first, made = barrier(held, [value for _, value in first], made)
    whole.update(zip(late, held))
    first = [([mask], value) for mask, value in zip(early, first)]
    last = pass_on(late)
    made = finish([(mask, whole[mask]) for mask in late if mask not in soon], first, tuple(made))
    return tuple(finish([], [last], tuple(made)))


def solution(mesh):
    inner, outer = mesh.shape["inner"], mesh.shape["outer"]
    x = inner // 2
    y = x if outer % x == 0 else 1
    z = outer // y
    zl = 2 if z % 2 == 0 else 1
    whole = Mesh(mesh.devices.reshape(x, 2, z // zl, zl, y), ("x", "core", "zh", "zl", "y"))
    rows = ("zh", "zl", "y", "x", "core")
    return jax.shard_map(
        shards,
        mesh=whole,
        in_specs=(P(rows, None),) * 4 + (P(rows),),
        out_specs=(P(rows, None),) * 4,
        check_vma=False,
    )
```

```python
import functools
import itertools
import math

import jax
import jax.numpy as jnp
from jax import lax
from jax.experimental import pallas as pl
from jax.experimental.pallas import tpu as pltpu
from jax.sharding import Mesh, PartitionSpec as P

D = 128
F32 = jnp.float32
BF16 = jnp.bfloat16
VMEM_LIMIT = 20 * 1024 * 1024
HBM = pl.BlockSpec(memory_space=pltpu.HBM)
VMEM = pl.BlockSpec(memory_space=pltpu.VMEM)
SMEM = pl.BlockSpec(memory_space=pltpu.SMEM)


def in_vmem(shape, dtype=F32):
    return pltpu.VMEM(shape, dtype)


def call(body, out_shape, in_specs, out_specs, scratch, flops, moved, name, aliases=None):
    return pl.pallas_call(
        body,
        out_shape=out_shape,
        in_specs=in_specs,
        out_specs=out_specs,
        scratch_shapes=scratch,
        input_output_aliases=aliases or {},
        compiler_params=pltpu.CompilerParams(vmem_limit_bytes=VMEM_LIMIT),
        cost_estimate=pl.CostEstimate(flops=flops, bytes_accessed=moved, transcendentals=0),
        name=name,
    )


def rotate(rows, cosine, sine):
    wide = rows.astype(F32)
    return wide * cosine + pltpu.roll(wide, D // 2, 1) * sine


def unrotate(rows, cosine, sine):
    return rows * cosine - pltpu.roll(rows, D // 2, 1) * sine


def dot(a, b, ca, cb):
    return lax.dot_general(a, b, (((ca,), (cb,)), ((), ())), preferred_element_type=F32)


def rotary_tables(positions):
    rows = positions.shape[1]
    half = D // 2
    index = lax.broadcasted_iota(jnp.int32, (half, rows), 0).astype(F32)
    frequency = jnp.exp(index * (-2.0 * math.log(500000.0) / D))
    angle = positions.astype(F32) * frequency
    cosine, sine = jnp.cos(angle), jnp.sin(angle)
    return jnp.concatenate([cosine, cosine], 0).T, jnp.concatenate([-sine, sine], 0).T


def states_body(first, per, sets, _, me, __, core, *refs):
    half, me = core[0], me[0]
    if first:
        pos, *sources = refs[:5]
        cos_ref, sin_ref, *fetched = refs[5:15]
        inputs, nearby = fetched[:4], fetched[4:]
        outs, place, sems = refs[15:17], refs[17], refs[18]
        width = inputs[0].shape[1]
        pos_copy = pltpu.make_async_copy(pos, place, sems.at[8])
        pos_copy.start()
        copies = []
        for n, (at, targets) in enumerate(((1 - half, inputs), (half, nearby))):
            start = pl.multiple_of(at * width, width)
            for i, (source, target) in enumerate(zip(sources, targets)):
                copies.append(pltpu.make_async_copy(source.at[:, pl.ds(start, width)], target, sems.at[4 * n + i]))
                copies[-1].start()
        pos_copy.wait()
        cosine, sine = rotary_tables(place[...])
        cos_ref[...] = cosine
        sin_ref[...] = sine
    else:
        cos_ref, sin_ref, *inputs = refs[:6]
        outs = refs[6:]
        cosine, sine = cos_ref[...], sin_ref[...]
    low = me % per
    for side in range(2):
        rows, others = inputs[2 * side : 2 * side + 2]
        if first:
            copies[2 * side].wait()
            copies[2 * side + 1].wait()
        for group, out in zip(sets, outs):
            cut = out.shape[2]
            for n, mask in enumerate(group):
                cols = pl.ds(pl.multiple_of(((me // per) ^ mask) * D, D), D)
                turned = rotate(rows[:, cols], cosine, sine).astype(BF16)
                state = dot(turned, others[:, cols], 0, 0)
                for i in range(per):
                    out[n * per + (low ^ i), side] = state[i * cut : (i + 1) * cut]
    if first:
        for copy in copies[4:]:
            copy.wait()


def states(who, first, per, sets, sources, tables_or_pos):
    rows, width = sources[0].shape
    heads = sum(map(len, sets))
    table = in_vmem((rows, D))
    results = [in_vmem((len(group) * per, 2, D // per, D)) for group in sets]
    body = functools.partial(states_body, first, per, sets)
    work = (4 * heads * rows * D * D, heads * D * (8 * rows + 8 * D))
    if first:
        piece = (rows, heads * D)
        scratch = [pltpu.VMEM((1, rows), jnp.int32), pltpu.SemaphoreType.DMA((9,))]
        out = call(
            body, [table] * 2 + [in_vmem(piece, BF16)] * 8 + results, [SMEM] * 4 + [HBM] * 5, [VMEM] * 12,
            scratch, *work, "block_states",
        )(*who, tables_or_pos, *sources)
        return out[:2], out[2:6], out[6:10], out[10:]
    return call(body, results, [SMEM] * 4 + [VMEM] * 6, [VMEM] * 2, [], *work, "block_states")(
        *who, *tables_or_pos, *sources
    )


def add_body(a_ref, b_ref, *pieces):
    for n, piece in enumerate(pieces):
        piece[...] = a_ref[n] + b_ref[n]


def add(a, b):
    count, _, cut, _ = a.shape
    return call(
        add_body, [in_vmem((2, cut, D))] * count, [VMEM] * 2, [VMEM] * count, [], a.size, a.size * 12, "chip_sum",
    )(a, b)


def total_body(_, __, group, ___, *refs):
    group = group[0]
    out_ref = refs[-1]
    for side in range(2):
        total = refs[0][side]
        for ref in refs[1:-1]:
            total = total + ref[side]
        if out_ref.shape[0] == 2:
            out_ref[side] = total
        elif side == 0:
            keys = total
        else:
            out_ref[0] = jnp.where(group == 0, keys, total)


def total(who, pieces, kinds):
    _, cut, _ = pieces[0].shape
    size = len(pieces) * pieces[0].size
    return call(
        total_body, in_vmem((kinds, cut, D)), [SMEM] * 4 + [VMEM] * len(pieces), VMEM, [], size, size * 4, "block_total",
    )(*who, *pieces)


def offset_body(members, _, __, group, ___, passed_ref, *refs):
    group = group[0]
    for side in range(2):
        if passed_ref.shape[0] == 1:
            extra = jnp.where(group == 1 - side, passed_ref[0], 0.0)
        else:
            extra = passed_ref[side]
        for m in range(members):
            refs[members + m][side] = refs[m][side] + extra


def offset(who, sums, passed):
    members = len(sums)
    size = members * sums[0].size
    return call(
        functools.partial(offset_body, members), [in_vmem(sums[0].shape)] * members,
        [SMEM] * 4 + [VMEM] * (members + 1), [VMEM] * members, [], size, size * 8, "group_sum",
    )(*who, passed, *sums)


def scan_body(members, _, me, __, ___, *refs):
    pieces, sums, (held, ran) = refs[:members], refs[members : 2 * members], refs[2 * members :]
    me = me[0]
    for m in range(members):
        held[me ^ m] = pieces[m][...]
    for side, order in enumerate((range(members), reversed(range(members)))):
        total = jnp.zeros(held.shape[2:], F32)
        for j in order:
            ran[j, side] = total
            total = total + held[j, side]
    for m in range(members):
        sums[m][...] = ran[me ^ m]


def scan(who, pieces):
    members, (_, cut, _) = len(pieces), pieces[0].shape
    shape = (members, 2, cut, D)
    size = math.prod(shape)
    return call(
        functools.partial(scan_body, members), [in_vmem((2, cut, D))] * members,
        [SMEM] * 4 + [VMEM] * members, [VMEM] * members, [pltpu.VMEM(shape, F32)] * 2, size, size * 8, "chip_scan",
    )(*who, *pieces)


def local_body(*refs):
    halves, (cos_ref, sin_ref, rot_ref, part_ref, sc_ref) = (refs[:4], refs[4:8]), refs[8:]
    cosine, sine = cos_ref[...], sin_ref[...]
    rows = cosine.shape[0]
    row = lax.broadcasted_iota(jnp.int32, (rows, rows), 0)
    col = lax.broadcasted_iota(jnp.int32, (rows, rows), 1)
    heads = rot_ref.shape[0]

    def scores(a, b, kept):
        return jnp.where(kept, dot(a, b, 1, 1), 0.0).astype(BF16)

    for h in range(heads):
        k_ref, v_ref, q_ref, g_ref = halves[h // (heads // 2)]
        cols = slice(h % (heads // 2) * D, (h % (heads // 2) + 1) * D)
        krot = rotate(k_ref[:, cols], cosine, sine).astype(BF16)
        qrot = rotate(q_ref[:, cols], cosine, sine).astype(BF16)
        v, g = v_ref[:, cols], g_ref[:, cols]
        for i, value in enumerate((qrot, g, v, krot)):
            rot_ref[h, i] = value
        sc_ref[h, 0] = scores(qrot, krot, row >= col)
        sc_ref[h, 1] = scores(g, v, row >= col)
        sc_ref[h, 2] = scores(v, g, row <= col)
        sc_ref[h, 3] = scores(krot, qrot, row <= col)
    for h in range(heads):
        for i, other in enumerate((2, 3, 0, 1)):
            part_ref[h, i] = dot(sc_ref[h, i], rot_ref[h, other], 1, 0)


def local_parts(near, far, tables, heads):
    rows = near[0].shape[0]
    return call(
        local_body,
        [in_vmem((heads, 4, rows, D), BF16), in_vmem((heads, 4, rows, D))],
        [VMEM] * 10, [VMEM] * 2, [pltpu.VMEM((heads, 4, rows, rows), BF16)], 16 * heads * rows * D * D,
        16 * rows * heads * D * 2, "local_parts",
    )(*near, *far, *tables)


def outputs_body(scale, per, jobs, arrays, prior, spots, core, me, _, __, rot_ref, part_ref, cos_ref, sin_ref, *refs):
    core, me = core[0], me[0]
    extras, pieces, refs = refs[:2], refs[2 : 2 + arrays], refs[2 + arrays + prior :]
    outs, (state_ref, held, sems) = refs[:4], refs[4:]
    cosine, sine = cos_ref[...], sin_ref[...]
    half = rot_ref.shape[0] // 2
    copies = []
    for n, (mask, mine, first, spot) in enumerate(jobs):
        low = me % per
        head = (me // per) ^ mask
        for i in range(per):
            cut = pieces[0].shape[-2]
            at = pl.ds(pl.multiple_of((low ^ i) * cut, cut), cut)
            for side in range(2):
                if mine:
                    which, kept = spots[mask]
                    extra = extras[which][kept * per + i, side]
                    state = pieces[first + i][side] + jnp.where(core == 1 - side, extra, 0.0)
                else:
                    state = pieces[first][spot * per + i, side]
                state_ref[n, side, at] = state.astype(BF16)
        before, after = state_ref[n, 0], state_ref[n, 1]
        at = head if mine else half + head
        att = part_ref[at, 0] + dot(rot_ref[at, 0], before, 1, 0)
        rqg = part_ref[at, 1] + dot(rot_ref[at, 1], before, 1, 1)
        rkg = part_ref[at, 2] + dot(rot_ref[at, 2], after, 1, 1)
        vg = part_ref[at, 3] + dot(rot_ref[at, 3], after, 1, 0)
        held[n, 0] = (scale * att).astype(BF16)
        held[n, 1] = unrotate(scale * rqg, cosine, sine).astype(BF16)
        held[n, 2] = unrotate(scale * rkg, cosine, sine).astype(BF16)
        held[n, 3] = (scale * vg).astype(BF16)
        column = ((core if mine else 1 - core) * half + head) * D
        for i in range(4):
            cols = pl.ds(pl.multiple_of(column, D), D)
            copies.append(pltpu.make_async_copy(held.at[n, i], outs[i].at[:, cols], sems.at[n, i]))
            copies[-1].start()
    for copy in copies:
        copy.wait()


def outputs(scale, per, spots, who, rot, local, tables, kept, own, far, prior):
    heads, _, rows, _ = rot.shape
    jobs, pieces = [], []
    for mask, values in own:
        jobs.append((mask, True, len(pieces), 0))
        pieces += values
    for masks, value in far:
        jobs += [(mask, False, len(pieces), spot) for spot, mask in enumerate(masks)]
        pieces.append(value)
    count = len(jobs)
    return call(
        functools.partial(outputs_body, scale, per, jobs, len(pieces), len(prior), spots),
        [pltpu.HBM((rows, heads * D), BF16)] * 4,
        [SMEM] * 4 + [VMEM] * (6 + len(pieces)) + [HBM] * len(prior),
        [HBM] * 4,
        [
            pltpu.VMEM((count, 2, D, D), BF16),
            pltpu.VMEM((count, 4, rows, D), BF16),
            pltpu.SemaphoreType.DMA((count, 4)),
        ],
        8 * count * rows * D * D,
        16 * rows * count * D * 2,
        "block_outputs",
        {10 + len(pieces) + i: i for i in range(len(prior))},
    )(*who, rot, local, *tables, *kept, *pieces, *prior)


def relay_body(per, masks, spots, core, _, __, ___, near_1, near_2, *refs):
    core = core[0]
    out_ref = refs[-1]
    for n, mask in enumerate(masks):
        which, spot = spots[mask]
        near = (near_1, near_2)[which]
        for i in range(per):
            for side in range(2):
                extra = jnp.where(core == side, near[spot * per + i, side], 0.0)
                out_ref[n * per + i, side] = refs[n * per + i][side] + extra


def relay(per, masks, spots, who, near, pieces):
    size = len(pieces) * pieces[0].size
    return call(
        functools.partial(relay_body, per, masks, spots), in_vmem((len(pieces),) + pieces[0].shape),
        [SMEM] * 4 + [VMEM] * (2 + len(pieces)), VMEM, [], size, size * 8, "sibling_state",
    )(*who, *near, *pieces)


def swap(value, axis):
    return lax.ppermute(value, axis, [(0, 1), (1, 0)])


AXES = ("x", "zl", "y")


def send_to(value, mask):
    x, zl, y = (lax.axis_size(axis) for axis in AXES)
    mx, my, mz = mask % x, mask // x % y, mask // (x * y)
    place = lambda a, b, c: (a * zl + b) * y + c
    pairs = [
        (place(a, b, c), place(a ^ mx, b ^ mz, c ^ my))
        for a, b, c in itertools.product(range(x), range(zl), range(y))
    ]
    return lax.ppermute(value, AXES, pairs)


def barrier(*values):
    return lax.optimization_barrier(values)


def exchange(pieces, order):
    arrived = {m: send_to(pieces[m], m) for m in order}
    arrived[0] = pieces[0]
    return arrived


def shards(q, k, v, g, positions):
    rows, width = q.shape
    heads = width // D
    part = heads // 2
    tokens = rows
    for axis in ("x", "core", "zh", "zl", "y"):
        tokens = tokens * lax.axis_size(axis)
    scale = (D * tokens) ** (-0.5)
    core, group = lax.axis_index("core"), lax.axis_index("zh")
    members, groups = lax.axis_size(("zl", "y", "x")), lax.axis_size("zh")
    me = lax.axis_index(("zl", "y", "x"))
    who = [scalar.reshape(1) for scalar in (core, me, group, core)]
    per = members // part
    pos = positions.reshape(1, rows)

    short = sorted(range(1, members - 1), key=lambda m: (bin(m).count("1"), m))[: members // 2 - 1]
    order = [route for m in short[:-1] for route in (m, members - 1 - m)]
    order += [members - 1 - short[-1], short[-1], members - 1]
    back = [route for m in short[:1] + short[:0:-1] for route in (m, members - 1 - m)] + [members - 1]
    masks = list(dict.fromkeys([m // per for m in order] + [0]))
    sets = masks[: part // 2], masks[part // 2 :]
    spots = {mask: (which, group.index(mask)) for which, group in enumerate(sets) for mask in group}

    sources = [pltpu.with_memory_space_constraint(a, pltpu.HBM) for a in (k, v, q, g)]
    tables, faraway, nearby, far = states(who, True, per, sets, sources, pltpu.with_memory_space_constraint(pos, pltpu.HBM))
    near = states(who, False, per, sets, nearby, tables)
    held_back, near = barrier(far[1], near)
    near_other = [swap(far[0], "core"), swap(held_back, "core")]
    summed = [add(*pair) for pair in zip(near, near_other)]
    pieces = {mask * per + i: summed[which][n * per + i] for mask, (which, n) in spots.items() for i in range(per)}
    pieces = [pieces[m] for m in range(members)]
    pieces[order[0]], tables = barrier(pieces[order[0]], tables)
    arrived = exchange(pieces, order)
    rot, local = local_parts(nearby, faraway, tables, heads)
    listed, rot, local = barrier([arrived[m] for m in order], rot, local)
    arrived = [pieces[0]] + [listed[order.index(m)] for m in range(1, members)]

    send = total(who, arrived, 1 if groups == 2 else 2)
    if groups == 2:
        passed = swap(send, "zh")
    else:
        every = lax.all_gather(send, "zh")
        place = jnp.arange(groups)[:, None, None, None]
        wanted = jnp.where(jnp.arange(2)[:, None, None] == 0, place < group, place > group)
        passed = jnp.sum(jnp.where(wanted, every, 0.0), axis=0)
    pieces = offset(who, scan(who, arrived), passed)
    whole = exchange(pieces, back)

    whole = {mask: [whole[mask * per + i] for i in range(per)] for mask in masks}

    def pass_on(chosen):
        listed = [piece for mask in chosen for piece in whole[mask]]
        return chosen, swap(relay(per, chosen, spots, who, near, listed), "core")

    returned = list(dict.fromkeys([m // per for m in back] + [0]))
    early, late = returned[: part // 2], returned[part // 2 :]
    soon = list(dict.fromkeys([0, *early]))
    first = [pass_on([mask]) for mask in early]
    finish = functools.partial(outputs, scale, per, spots, who, rot, local, tables, near_other)
    made = finish([(mask, whole[mask]) for mask in soon], [], ())
    held = [whole[mask] for mask in late]
    held, first, made = barrier(held, [value for _, value in first], made)
    whole.update(zip(late, held))
    first = [([mask], value) for mask, value in zip(early, first)]
    last = pass_on(late)
    made = finish([(mask, whole[mask]) for mask in late if mask not in soon], first, tuple(made))
    return tuple(finish([], [last], tuple(made)))


def solution(mesh):
    inner, outer = mesh.shape["inner"], mesh.shape["outer"]
    x = inner // 2
    y = x if outer % x == 0 else 1
    z = outer // y
    zl = 2 if z % 2 == 0 else 1
    whole = Mesh(mesh.devices.reshape(x, 2, z // zl, zl, y), ("x", "core", "zh", "zl", "y"))
    rows = ("zh", "zl", "y", "x", "core")
    return jax.shard_map(
        shards,
        mesh=whole,
        in_specs=(P(rows, None),) * 4 + (P(rows),),
        out_specs=(P(rows, None),) * 4,
        check_vma=False,
    )
```

```python
import functools
import itertools
import math

import jax
import jax.numpy as jnp
from jax import lax
from jax.experimental import pallas as pl
from jax.experimental.pallas import tpu as pltpu
from jax.sharding import Mesh, PartitionSpec as P

D = 128
F32 = jnp.float32
BF16 = jnp.bfloat16
VMEM_LIMIT = 20 * 1024 * 1024
HBM = pl.BlockSpec(memory_space=pltpu.HBM)
VMEM = pl.BlockSpec(memory_space=pltpu.VMEM)
SMEM = pl.BlockSpec(memory_space=pltpu.SMEM)


def in_vmem(shape, dtype=F32):
    return pltpu.VMEM(shape, dtype)


def call(body, out_shape, in_specs, out_specs, scratch, flops, moved, name, aliases=None):
    return pl.pallas_call(
        body,
        out_shape=out_shape,
        in_specs=in_specs,
        out_specs=out_specs,
        scratch_shapes=scratch,
        input_output_aliases=aliases or {},
        compiler_params=pltpu.CompilerParams(vmem_limit_bytes=VMEM_LIMIT),
        cost_estimate=pl.CostEstimate(flops=flops, bytes_accessed=moved, transcendentals=0),
        name=name,
    )


def rotate(rows, cosine, sine):
    wide = rows.astype(F32)
    return wide * cosine + pltpu.roll(wide, D // 2, 1) * sine


def unrotate(rows, cosine, sine):
    return rows * cosine - pltpu.roll(rows, D // 2, 1) * sine


def dot(a, b, ca, cb):
    return lax.dot_general(a, b, (((ca,), (cb,)), ((), ())), preferred_element_type=F32)


def rotary_tables(positions):
    rows = positions.shape[1]
    half = D // 2
    index = lax.broadcasted_iota(jnp.int32, (half, rows), 0).astype(F32)
    frequency = jnp.exp(index * (-2.0 * math.log(500000.0) / D))
    angle = positions.astype(F32) * frequency
    cosine, sine = jnp.cos(angle), jnp.sin(angle)
    return jnp.concatenate([cosine, cosine], 0).T, jnp.concatenate([-sine, sine], 0).T


def states_body(first, per, sets, _, me, __, core, *refs):
    half, me = core[0], me[0]
    if first:
        pos, *sources = refs[:5]
        cos_ref, sin_ref, *fetched = refs[5:15]
        inputs, nearby = fetched[:4], fetched[4:]
        outs, place, sems = refs[15:17], refs[17], refs[18]
        width = inputs[0].shape[1]
        pos_copy = pltpu.make_async_copy(pos, place, sems.at[8])
        pos_copy.start()
        copies = []
        for n, (at, targets) in enumerate(((1 - half, inputs), (half, nearby))):
            start = pl.multiple_of(at * width, width)
            for i, (source, target) in enumerate(zip(sources, targets)):
                copies.append(pltpu.make_async_copy(source.at[:, pl.ds(start, width)], target, sems.at[4 * n + i]))
                copies[-1].start()
        pos_copy.wait()
        cosine, sine = rotary_tables(place[...])
        cos_ref[...] = cosine
        sin_ref[...] = sine
    else:
        cos_ref, sin_ref, *inputs = refs[:6]
        outs = refs[6:]
        cosine, sine = cos_ref[...], sin_ref[...]
    low = me % per
    for side in range(2):
        rows, others = inputs[2 * side : 2 * side + 2]
        if first:
            copies[2 * side].wait()
            copies[2 * side + 1].wait()
        for group, out in zip(sets, outs):
            cut = out.shape[2]
            for n, mask in enumerate(group):
                cols = pl.ds(pl.multiple_of(((me // per) ^ mask) * D, D), D)
                turned = rotate(rows[:, cols], cosine, sine).astype(BF16)
                state = dot(turned, others[:, cols], 0, 0)
                for i in range(per):
                    out[n * per + (low ^ i), side] = state[i * cut : (i + 1) * cut]
    if first:
        for copy in copies[4:]:
            copy.wait()


def states(who, first, per, sets, sources, tables_or_pos):
    rows, width = sources[0].shape
    heads = sum(map(len, sets))
    table = in_vmem((rows, D))
    results = [in_vmem((len(group) * per, 2, D // per, D)) for group in sets]
    body = functools.partial(states_body, first, per, sets)
    work = (4 * heads * rows * D * D, heads * D * (8 * rows + 8 * D))
    if first:
        piece = (rows, heads * D)
        scratch = [pltpu.VMEM((1, rows), jnp.int32), pltpu.SemaphoreType.DMA((9,))]
        out = call(
            body, [table] * 2 + [in_vmem(piece, BF16)] * 8 + results, [SMEM] * 4 + [HBM] * 5, [VMEM] * 12,
            scratch, *work, "block_states",
        )(*who, tables_or_pos, *sources)
        return out[:2], out[2:6], out[6:10], out[10:]
    return call(body, results, [SMEM] * 4 + [VMEM] * 6, [VMEM] * 2, [], *work, "block_states")(
        *who, *tables_or_pos, *sources
    )


def add_body(a_ref, b_ref, *pieces):
    for n, piece in enumerate(pieces):
        piece[...] = a_ref[n] + b_ref[n]


def add(a, b):
    count, _, cut, _ = a.shape
    return call(
        add_body, [in_vmem((2, cut, D))] * count, [VMEM] * 2, [VMEM] * count, [], a.size, a.size * 12, "chip_sum",
    )(a, b)


def total_body(_, __, group, ___, *refs):
    group = group[0]
    out_ref = refs[-1]
    for side in range(2):
        total = refs[0][side]
        for ref in refs[1:-1]:
            total = total + ref[side]
        if out_ref.shape[0] == 2:
            out_ref[side] = total
        elif side == 0:
            keys = total
        else:
            out_ref[0] = jnp.where(group == 0, keys, total)


def total(who, pieces, kinds):
    _, cut, _ = pieces[0].shape
    size = len(pieces) * pieces[0].size
    return call(
        total_body, in_vmem((kinds, cut, D)), [SMEM] * 4 + [VMEM] * len(pieces), VMEM, [], size, size * 4, "block_total",
    )(*who, *pieces)


def offset_body(members, _, __, group, ___, passed_ref, *refs):
    group = group[0]
    for side in range(2):
        if passed_ref.shape[0] == 1:
            extra = jnp.where(group == 1 - side, passed_ref[0], 0.0)
        else:
            extra = passed_ref[side]
        for m in range(members):
            refs[members + m][side] = refs[m][side] + extra


def offset(who, sums, passed):
    members = len(sums)
    size = members * sums[0].size
    return call(
        functools.partial(offset_body, members), [in_vmem(sums[0].shape)] * members,
        [SMEM] * 4 + [VMEM] * (members + 1), [VMEM] * members, [], size, size * 8, "group_sum",
    )(*who, passed, *sums)


def scan_body(members, _, me, __, ___, *refs):
    pieces, sums, (held, ran) = refs[:members], refs[members : 2 * members], refs[2 * members :]
    me = me[0]
    for m in range(members):
        held[me ^ m] = pieces[m][...]
    for side, order in enumerate((range(members), reversed(range(members)))):
        total = jnp.zeros(held.shape[2:], F32)
        for j in order:
            ran[j, side] = total
            total = total + held[j, side]
    for m in range(members):
        sums[m][...] = ran[me ^ m]


def scan(who, pieces):
    members, (_, cut, _) = len(pieces), pieces[0].shape
    shape = (members, 2, cut, D)
    size = math.prod(shape)
    return call(
        functools.partial(scan_body, members), [in_vmem((2, cut, D))] * members,
        [SMEM] * 4 + [VMEM] * members, [VMEM] * members, [pltpu.VMEM(shape, F32)] * 2, size, size * 8, "chip_scan",
    )(*who, *pieces)


def local_body(*refs):
    halves, (cos_ref, sin_ref, rot_ref, part_ref, sc_ref) = (refs[:4], refs[4:8]), refs[8:]
    cosine, sine = cos_ref[...], sin_ref[...]
    rows = cosine.shape[0]
    row = lax.broadcasted_iota(jnp.int32, (rows, rows), 0)
    col = lax.broadcasted_iota(jnp.int32, (rows, rows), 1)
    heads = rot_ref.shape[0]

    def scores(a, b, kept):
        return jnp.where(kept, dot(a, b, 1, 1), 0.0).astype(BF16)

    for h in range(heads):
        k_ref, v_ref, q_ref, g_ref = halves[h // (heads // 2)]
        cols = slice(h % (heads // 2) * D, (h % (heads // 2) + 1) * D)
        krot = rotate(k_ref[:, cols], cosine, sine).astype(BF16)
        qrot = rotate(q_ref[:, cols], cosine, sine).astype(BF16)
        v, g = v_ref[:, cols], g_ref[:, cols]
        for i, value in enumerate((qrot, g, v, krot)):
            rot_ref[h, i] = value
        sc_ref[h, 0] = scores(qrot, krot, row >= col)
        sc_ref[h, 1] = scores(g, v, row >= col)
        sc_ref[h, 2] = scores(v, g, row <= col)
        sc_ref[h, 3] = scores(krot, qrot, row <= col)
    for h in range(heads):
        for i, other in enumerate((2, 3, 0, 1)):
            part_ref[h, i] = dot(sc_ref[h, i], rot_ref[h, other], 1, 0)


def local_parts(near, far, tables, heads):
    rows = near[0].shape[0]
    return call(
        local_body,
        [in_vmem((heads, 4, rows, D), BF16), in_vmem((heads, 4, rows, D))],
        [VMEM] * 10, [VMEM] * 2, [pltpu.VMEM((heads, 4, rows, rows), BF16)], 16 * heads * rows * D * D,
        16 * rows * heads * D * 2, "local_parts",
    )(*near, *far, *tables)


def outputs_body(scale, per, jobs, arrays, prior, spots, core, me, _, __, rot_ref, part_ref, cos_ref, sin_ref, *refs):
    core, me = core[0], me[0]
    extras, pieces, refs = refs[:2], refs[2 : 2 + arrays], refs[2 + arrays + prior :]
    outs, (state_ref, held, sems) = refs[:4], refs[4:]
    cosine, sine = cos_ref[...], sin_ref[...]
    half = rot_ref.shape[0] // 2
    copies = []
    for n, (mask, mine, first, spot) in enumerate(jobs):
        low = me % per
        head = (me // per) ^ mask
        for i in range(per):
            cut = pieces[0].shape[-2]
            at = pl.ds(pl.multiple_of((low ^ i) * cut, cut), cut)
            for side in range(2):
                if mine:
                    which, kept = spots[mask]
                    extra = extras[which][kept * per + i, side]
                    state = pieces[first + i][side] + jnp.where(core == 1 - side, extra, 0.0)
                else:
                    state = pieces[first][spot * per + i, side]
                state_ref[n, side, at] = state.astype(BF16)
        before, after = state_ref[n, 0], state_ref[n, 1]
        at = head if mine else half + head
        att = part_ref[at, 0] + dot(rot_ref[at, 0], before, 1, 0)
        rqg = part_ref[at, 1] + dot(rot_ref[at, 1], before, 1, 1)
        rkg = part_ref[at, 2] + dot(rot_ref[at, 2], after, 1, 1)
        vg = part_ref[at, 3] + dot(rot_ref[at, 3], after, 1, 0)
        held[n, 0] = (scale * att).astype(BF16)
        held[n, 1] = unrotate(scale * rqg, cosine, sine).astype(BF16)
        held[n, 2] = unrotate(scale * rkg, cosine, sine).astype(BF16)
        held[n, 3] = (scale * vg).astype(BF16)
        column = ((core if mine else 1 - core) * half + head) * D
        for i in range(4):
            cols = pl.ds(pl.multiple_of(column, D), D)
            copies.append(pltpu.make_async_copy(held.at[n, i], outs[i].at[:, cols], sems.at[n, i]))
            copies[-1].start()
    for copy in copies:
        copy.wait()


def outputs(scale, per, spots, who, rot, local, tables, kept, own, far, prior):
    heads, _, rows, _ = rot.shape
    jobs, pieces = [], []
    for mask, values in own:
        jobs.append((mask, True, len(pieces), 0))
        pieces += values
    for masks, value in far:
        jobs += [(mask, False, len(pieces), spot) for spot, mask in enumerate(masks)]
        pieces.append(value)
    count = len(jobs)
    return call(
        functools.partial(outputs_body, scale, per, jobs, len(pieces), len(prior), spots),
        [pltpu.HBM((rows, heads * D), BF16)] * 4,
        [SMEM] * 4 + [VMEM] * (6 + len(pieces)) + [HBM] * len(prior),
        [HBM] * 4,
        [
            pltpu.VMEM((count, 2, D, D), BF16),
            pltpu.VMEM((count, 4, rows, D), BF16),
            pltpu.SemaphoreType.DMA((count, 4)),
        ],
        8 * count * rows * D * D,
        16 * rows * count * D * 2,
        "block_outputs",
        {10 + len(pieces) + i: i for i in range(len(prior))},
    )(*who, rot, local, *tables, *kept, *pieces, *prior)


def relay_body(per, masks, spots, core, _, __, ___, near_1, near_2, *refs):
    core = core[0]
    out_ref = refs[-1]
    for n, mask in enumerate(masks):
        which, spot = spots[mask]
        near = (near_1, near_2)[which]
        for i in range(per):
            for side in range(2):
                extra = jnp.where(core == side, near[spot * per + i, side], 0.0)
                out_ref[n * per + i, side] = refs[n * per + i][side] + extra


def relay(per, masks, spots, who, near, pieces):
    size = len(pieces) * pieces[0].size
    return call(
        functools.partial(relay_body, per, masks, spots), in_vmem((len(pieces),) + pieces[0].shape),
        [SMEM] * 4 + [VMEM] * (2 + len(pieces)), VMEM, [], size, size * 8, "sibling_state",
    )(*who, *near, *pieces)


def swap(value, axis):
    return lax.ppermute(value, axis, [(0, 1), (1, 0)])


AXES = ("x", "zl", "y")


def send_to(value, mask):
    x, zl, y = (lax.axis_size(axis) for axis in AXES)
    mx, my, mz = mask % x, mask // x % y, mask // (x * y)
    place = lambda a, b, c: (a * zl + b) * y + c
    pairs = [
        (place(a, b, c), place(a ^ mx, b ^ mz, c ^ my))
        for a, b, c in itertools.product(range(x), range(zl), range(y))
    ]
    return lax.ppermute(value, AXES, pairs)


def barrier(*values):
    return lax.optimization_barrier(values)


def exchange(pieces, order):
    arrived = {m: send_to(pieces[m], m) for m in order}
    arrived[0] = pieces[0]
    return arrived


def shards(q, k, v, g, positions):
    rows, width = q.shape
    heads = width // D
    part = heads // 2
    tokens = rows
    for axis in ("x", "core", "zh", "zl", "y"):
        tokens = tokens * lax.axis_size(axis)
    scale = (D * tokens) ** (-0.5)
    core, group = lax.axis_index("core"), lax.axis_index("zh")
    members, groups = lax.axis_size(("zl", "y", "x")), lax.axis_size("zh")
    me = lax.axis_index(("zl", "y", "x"))
    who = [scalar.reshape(1) for scalar in (core, me, group, core)]
    per = members // part
    pos = positions.reshape(1, rows)

    short = sorted(range(1, members - 1), key=lambda m: (bin(m).count("1"), m))[: members // 2 - 1]
    order = [route for m in short for route in (m, members - 1 - m)] + [members - 1]
    back = [route for m in short[:1] + short[:1:-1] for route in (m, members - 1 - m)]
    back += [members - 1 - short[1], short[1], members - 1]
    masks = list(dict.fromkeys([m // per for m in order] + [0]))
    sets = masks[: part // 2], masks[part // 2 :]
    spots = {mask: (which, group.index(mask)) for which, group in enumerate(sets) for mask in group}

    sources = [pltpu.with_memory_space_constraint(a, pltpu.HBM) for a in (k, v, q, g)]
    tables, faraway, nearby, far = states(who, True, per, sets, sources, pltpu.with_memory_space_constraint(pos, pltpu.HBM))
    near = states(who, False, per, sets, nearby, tables)
    held_back, near = barrier(far[1], near)
    near_other = [swap(far[0], "core"), swap(held_back, "core")]
    summed = [add(*pair) for pair in zip(near, near_other)]
    pieces = {mask * per + i: summed[which][n * per + i] for mask, (which, n) in spots.items() for i in range(per)}
    pieces = [pieces[m] for m in range(members)]
    pieces[order[0]], tables = barrier(pieces[order[0]], tables)
    arrived = exchange(pieces, order)
    rot, local = local_parts(nearby, faraway, tables, heads)
    listed, rot, local = barrier([arrived[m] for m in order], rot, local)
    arrived = [pieces[0]] + [listed[order.index(m)] for m in range(1, members)]

    send = total(who, arrived, 1 if groups == 2 else 2)
    if groups == 2:
        passed = swap(send, "zh")
    else:
        every = lax.all_gather(send, "zh")
        place = jnp.arange(groups)[:, None, None, None]
        wanted = jnp.where(jnp.arange(2)[:, None, None] == 0, place < group, place > group)
        passed = jnp.sum(jnp.where(wanted, every, 0.0), axis=0)
    pieces = offset(who, scan(who, arrived), passed)
    whole = exchange(pieces, back)

    whole = {mask: [whole[mask * per + i] for i in range(per)] for mask in masks}

    def pass_on(chosen):
        listed = [piece for mask in chosen for piece in whole[mask]]
        return chosen, swap(relay(per, chosen, spots, who, near, listed), "core")

    returned = list(dict.fromkeys([m // per for m in back] + [0]))
    early, late = returned[: part // 2], returned[part // 2 :]
    soon = list(dict.fromkeys([0, *early]))
    first = [pass_on([mask]) for mask in early]
    finish = functools.partial(outputs, scale, per, spots, who, rot, local, tables, near_other)
    made = finish([(mask, whole[mask]) for mask in soon], [], ())
    held = [whole[mask] for mask in late]
    held, first, made = barrier(held, [value for _, value in first], made)
    whole.update(zip(late, held))
    first = [([mask], value) for mask, value in zip(early, first)]
    last = pass_on(late)
    made = finish([(mask, whole[mask]) for mask in late if mask not in soon], first, tuple(made))
    return tuple(finish([], [last], tuple(made)))


def solution(mesh):
    inner, outer = mesh.shape["inner"], mesh.shape["outer"]
    x = inner // 2
    y = x if outer % x == 0 else 1
    z = outer // y
    zl = 2 if z % 2 == 0 else 1
    whole = Mesh(mesh.devices.reshape(x, 2, z // zl, zl, y), ("x", "core", "zh", "zl", "y"))
    rows = ("zh", "zl", "y", "x", "core")
    return jax.shard_map(
        shards,
        mesh=whole,
        in_specs=(P(rows, None),) * 4 + (P(rows),),
        out_specs=(P(rows, None),) * 4,
        check_vma=False,
    )
```
